1024 devices in a mesh: pipe: 4 (over y_hi), dp: 256 (over y_lo, z, x, core).
Axes of the slice: x: 4, y: 8 (y_hi: 4, y_lo: 2; y = y_hi * 2 + y_lo), z: 16, core: 2. Of those that a mesh axis runs over, the one named last changes fastest.
Arguments:
- top_grad: bfloat16 [32768, 8192], P('dp'), may hold values from -6 to 6
- slab_inputs: bfloat16 [4, 32768, 128], P('pipe', 'dp'), may hold values from -24 to 24
- weights: bfloat16 [4, 128, 8192], P('pipe'), may hold values from -0.0625 to 0.0625
- master: float32 [4, 8192, 128], P('pipe', 'dp'), may hold values from -0.01953125 to 0.01953125
- moment1: float32 [4, 8192, 128], P('pipe', 'dp'), may hold values from -0.00048828125 to 0.00048828125
- moment2: float32 [4, 8192, 128], P('pipe', 'dp'), may hold values from 1.1920929e-09 to 3.576279e-08
- grad_accum: float32 [4, 8192, 128], P('pipe', 'dp'), may hold values from -0.078125 to 0.078125
- layer_counts: int32 [4], replicated, may hold values from 4 to 36
Outputs:
- new_weights: bfloat16 [4, 128, 8192], P('pipe')
- adam_step: float32 [4, 8192, 128], P('pipe', 'dp')
- new_master: float32 [4, 8192, 128], P('pipe', 'dp')
- section_grads: bfloat16 [4, 32768, 128], P('pipe', 'dp')
The draws below stay inside these ranges and needn't reach their ends.
All inputs are finite; a program needn't handle non-finite values.
Results may differ from the reference program's by a relative error of at most 0.0027.
Values may be sent and summed in bfloat16 or wider, within the bound.
No kernel may reach another device: no remote copies, remote signals or barrier semaphores. Data moves between devices by JAX's collectives and lax.ppermute only.
A program may use at most 32 MiB of HBM per device.

```python
import math
import jax
import jax.numpy as jnp
from jax import lax

D = 8192
SLAB = 128
LANES = 128
TOKENS = 32768
FLAT = 8192
N_PIPE = 4


def plant(values, key, low, top_value):
    extent = values.shape
    spot = [jax.random.randint(jax.random.fold_in(key, axis), (), 0, extent[axis]) for axis in range(len(extent))]
    values = values.at[tuple(spot)].set(low)
    longest = extent.index(max(extent))
    spot[longest] = (spot[longest] + 1) % extent[longest]
    return values.at[tuple(spot)].set(top_value)


def strengthened(drawn, key, source, target, parts, factor):
    owner, partner = [(jnp.arange(drawn.shape[position]) // (drawn.shape[position] // parts)).reshape([-1 if axis == position else 1 for axis in range(drawn.ndim)]) for position in (source, target)]
    chosen = jax.random.permutation(key, parts)[partner]
    strong = (owner == chosen) | (owner == (partner + parts // 2) % parts)
    return jnp.where(strong, factor * drawn, drawn)


def levels(rng, extent, cuts, low, top_value):
    level = 1.0
    for dim, blocks in cuts:
        steps = jax.random.uniform(jax.random.fold_in(jax.random.fold_in(rng, 6), dim), (blocks,), jnp.float32, low / len(cuts), top_value / len(cuts))
        level = level * jnp.repeat(jnp.exp(steps), extent[dim] // blocks).reshape((-1,) + (1,) * (len(extent) - 1 - dim))
    return level


def scatter_about(stream_key, shape, deviation, most, pieces=(), kind=jnp.bfloat16):
    drawn = jax.random.normal(stream_key, shape, jnp.float32) * deviation
    if len(pieces) > 0:
        drawn = levels(stream_key, shape, pieces, -0.22, 0.18) * drawn
    return jnp.clip(drawn, min=-most, max=most).astype(kind)


def heavy_noise(key, shape, scale, most, pieces, heavy, dtype=jnp.bfloat16):
    entries = scale * jax.random.normal(key, shape, jnp.float32)
    if pieces:
        entries = entries * levels(key, shape, pieces, -0.22, 0.18)
    return jnp.clip(strengthened(entries, jax.random.fold_in(key, 3), *heavy), -most, most).astype(dtype)


def setup_inputs(seed: int = 0) -> dict:
    key_list = jax.random.split(jax.random.key(seed), 9)
    return {
        "top_grad": scatter_about(key_list[0], (TOKENS, D), 1.0, 6.0, ((0, 256),)),
        "slab_inputs": heavy_noise(key_list[1], (N_PIPE, TOKENS, SLAB), 1.0, 24.0, ((0, 4), (1, 256)), (1, 2, 128, 5.5)),
        "weights": scatter_about(key_list[2], (N_PIPE, SLAB, D), D ** -0.5, 0.0625, ((0, 4),)),
        "master": scatter_about(key_list[3], (N_PIPE, FLAT, LANES), (0.12 * D ** -0.5), 0.01953125, ((0, 4), (1, 256)), jnp.float32),
        "moment1": scatter_about(key_list[4], (N_PIPE, FLAT, LANES), (0.3 * (20 * N_PIPE * SLAB * D) ** -0.5), 0.00048828125, ((0, 4), (1, 256)), jnp.float32),
        "moment2": jnp.clip(jnp.exp(math.log(3.5762788286319847e-08) - 3.4011974 * jax.random.uniform(key_list[5], (N_PIPE, FLAT, LANES), jnp.float32) ** levels(key_list[5], (N_PIPE, FLAT, LANES), ((0, 4), (1, 256)), -0.2, 0.2)), 1.19209286886246e-09, 3.5762788286319847e-08),
        "grad_accum": scatter_about(key_list[6], (N_PIPE, FLAT, LANES), (TOKENS ** -0.5), 0.078125, ((0, 4), (1, 256)), jnp.float32),
        "layer_counts": plant(jax.random.randint(key_list[7], (N_PIPE,), 4, 37), jax.random.fold_in(key_list[7], 1), 4, 36).astype(jnp.int32),
    }


beta_one = 0.9
beta_two = 0.95
bias_one = 1.0 - 0.9 ** 20
bias_two = 1.0 - 0.95 ** 20
epsilon = 1e-08
decay_rate = 0.1
learn_rate = 0.0003
clip_norm = 1.0

def reference(top_grad, slab_inputs, weights, master, moment1, moment2, grad_accum, layer_counts):
    span_cols = N_PIPE * SLAB
    placed = jnp.zeros((TOKENS, span_cols), jnp.bfloat16)
    grads_out = [None] * N_PIPE
    last_grads = [None] * N_PIPE
    for section in range(N_PIPE - 1, -1, -1):
        head_cols = (top_grad[:, :span_cols].astype(jnp.float32) + placed.astype(jnp.float32)).astype(jnp.bfloat16)
        residual = jnp.concatenate([head_cols, top_grad[:, span_cols:]], axis=1)
        branch_grad = lax.dot_general(residual, weights[section], (((1,), (1,)), ((), ())), preferred_element_type=jnp.float32).astype(jnp.bfloat16)
        grads_out[section] = branch_grad
        weight_grad = lax.dot_general(slab_inputs[section], residual, (((0,), (0,)), ((), ())), preferred_element_type=jnp.float32) / TOKENS
        last_grads[section] = weight_grad.reshape(FLAT, LANES)
        placed = placed.at[:, section * SLAB:(section + 1) * SLAB].set(branch_grad)
    total_grad = grad_accum + jnp.stack(last_grads)
    square_norm = jnp.sum(layer_counts.astype(jnp.float32) * lax.optimization_barrier(jnp.sum(total_grad * total_grad, axis=(1, 2))))
    clip_factor = jnp.minimum(1.0, clip_norm / jnp.sqrt(square_norm))
    clipped = clip_factor * total_grad
    moment_one = beta_one * moment1 + (1.0 - beta_one) * clipped
    moment_two = beta_two * moment2 + (1.0 - beta_two) * clipped * clipped
    adam_step = moment_one / bias_one / (jnp.sqrt(moment_two / bias_two) + epsilon) + decay_rate * master
    new_master = master - learn_rate * adam_step
    new_weights = new_master.astype(jnp.bfloat16).reshape(N_PIPE, SLAB, D)
    return (new_weights, adam_step, new_master, jnp.stack(grads_out))
```

```python
import functools
import jax
import jax.numpy as jnp
from jax import lax
from jax.experimental import pallas as pl
from jax.experimental.pallas import tpu as pltpu
from jax.sharding import Mesh, PartitionSpec as P

beta_one = 0.9
beta_two = 0.95
bias_one = 1.0 - 0.9**20
bias_two = 1.0 - 0.95**20
epsilon = 1e-08
decay_rate = 0.1
learn_rate = 0.0003
clip_norm = 1.0

bf16 = jnp.bfloat16
f32 = jnp.float32
DP_AXES = ("y", "z", "x", "core")
DP_SIZES = (2, 16, 4, 2)


def dot(a, b, dims):
    return lax.dot_general(a, b, (dims, ((), ())), preferred_element_type=f32)


def vmem_spec():
    return pl.BlockSpec(memory_space=pltpu.VMEM)


def known_kernel(section_ref, top_ref, weight_ref, out_ref, *, slab, span):
    step = pl.program_id(0)

    @pl.when(step == 0)
    def _():
        column = lax.broadcasted_iota(jnp.int32, top_ref.shape, 1)
        later = (column >= (section_ref[0] + 1) * slab) & (column < span)
        known = jnp.where(later, 0.0, top_ref[...].astype(f32)).astype(bf16)
        out_ref[...] = dot(known, weight_ref[...], ((1,), (1,)))

    @pl.when(step != 0)
    def _():
        out_ref[...] += dot(top_ref[...], weight_ref[...], ((1,), (1,)))


def known_part(section, top_grad, weight, slab, span, steps):
    rows, width = top_grad.shape
    block = width // steps
    return pl.pallas_call(
        functools.partial(known_kernel, slab=slab, span=span),
        grid_spec=pltpu.PrefetchScalarGridSpec(
            num_scalar_prefetch=1,
            grid=(steps,),
            in_specs=[
                pl.BlockSpec((rows, block), lambda i, s: (0, i)),
                pl.BlockSpec((slab, block), lambda i, s: (0, i)),
            ],
            out_specs=pl.BlockSpec((rows, slab), lambda i, s: (0, 0)),
        ),
        out_shape=jax.ShapeDtypeStruct((rows, slab), f32),
        name="known_part",
    )(section, top_grad, weight)


def relay_kernel(section_ref, top_ref, own_ref, one_ref, two_ref, three_ref, w_own_ref, w_one_ref, w_two_ref, head_ref, grad_ref, *, slab):
    section = section_ref[0]
    known = (own_ref, one_ref, two_ref, three_ref)
    for u in range(3, -1, -1):
        @pl.when(section <= u)
        def _(u=u):
            offset = u - section
            total = known[3][...]
            for k in (2, 1, 0):
                total = jnp.where(offset == k, known[k][...], total)
            for v in range(u + 1, 4):
                block = slice(v * slab, (v + 1) * slab)
                weight = w_own_ref[:, block].astype(f32)
                if v >= 2:
                    narrow = slice((v - 2) * slab, (v - 1) * slab)
                    weight = jnp.where(offset == 1, w_one_ref[:, narrow].astype(f32), weight)
                    weight = jnp.where(offset == 2, w_two_ref[:, narrow].astype(f32), weight)
                total = total + dot(head_ref[:, block], weight.astype(bf16), ((1,), (1,)))
            branch = total.astype(bf16)
            here = slice(u * slab, (u + 1) * slab)
            top = top_ref[:, here]
            placed = (top.astype(f32) + branch.astype(f32)).astype(bf16)
            head_ref[:, here] = jnp.where(offset == 0, top.astype(f32), placed.astype(f32)).astype(bf16)
            grad_ref[...] = branch

        @pl.when(section > u)
        def _(u=u):
            here = slice(u * slab, (u + 1) * slab)
            head_ref[:, here] = top_ref[:, here]


def relay(section, top_head, known, weights, slab):
    rows, span = top_head.shape
    return pl.pallas_call(
        functools.partial(relay_kernel, slab=slab),
        in_specs=[pl.BlockSpec(memory_space=pltpu.SMEM)] + [vmem_spec()] * 8,
        out_specs=[vmem_spec()] * 2,
        out_shape=[
            jax.ShapeDtypeStruct((rows, span), bf16),
            jax.ShapeDtypeStruct((rows, slab), bf16),
        ],
        name="relay",
    )(section, top_head, *known, *weights)


def product_kernel(core_ref, order_ref, slab_a_ref, slab_b_ref, head_a_ref, head_b_ref, top_ref, other_ref, out_ref, a_ref, b_ref, *, span):
    step = pl.program_id(0)

    @pl.when(step == 0)
    def _():
        a_ref[...] = dot(order_ref[...], slab_a_ref[...], ((1,), (1,))).astype(bf16)
        b_ref[...] = dot(order_ref[...], slab_b_ref[...], ((1,), (1,))).astype(bf16)

    out_ref[...] = (
        dot(a_ref[...], top_ref[...], ((1,), (0,))) + dot(b_ref[...], other_ref[...], ((1,), (0,)))
    ).astype(bf16)

    @pl.when((step == 0) & (core_ref[0] == 0))
    def _():
        out_ref[:, :span] = (
            dot(a_ref[...], head_a_ref[...], ((1,), (0,))) + dot(b_ref[...], head_b_ref[...], ((1,), (0,)))
        ).astype(bf16)


def slab_product(core, order, slab_a, slab_b, head_a, head_b, top_grad, other, steps):
    rows = top_grad.shape[0]
    slab = slab_a.shape[1]
    half = top_grad.shape[1] // 2
    span = head_a.shape[1]
    block = half // steps
    whole = lambda shape: pl.BlockSpec(shape, lambda i, c: (0, 0))
    return pl.pallas_call(
        functools.partial(product_kernel, span=span),
        grid_spec=pltpu.PrefetchScalarGridSpec(
            num_scalar_prefetch=1,
            grid=(steps,),
            in_specs=[
                whole((slab, slab)),
                whole((rows, slab)),
                whole((rows, slab)),
                whole((rows, span)),
                whole((rows, span)),
                pl.BlockSpec((rows, block), lambda i, c: (0, c[0] * steps + i)),
                pl.BlockSpec((rows, block), lambda i, c: (0, i)),
            ],
            out_specs=pl.BlockSpec((slab, block), lambda i, c: (0, i)),
            scratch_shapes=[pltpu.VMEM((slab, rows), bf16), pltpu.VMEM((slab, rows), bf16)],
        ),
        out_shape=jax.ShapeDtypeStruct((slab, half), bf16),
        name="slab_product",
    )(core, order, slab_a, slab_b, head_a, head_b, top_grad, other)


def fold_kernel(parts_ref, out_ref, *, count):
    total = parts_ref[0].astype(f32)
    for i in range(1, count):
        total = total + parts_ref[i].astype(f32)
    out_ref[...] = total.astype(out_ref.dtype)


def fold(parts, dtype):
    return pl.pallas_call(
        functools.partial(fold_kernel, count=parts.shape[0]),
        in_specs=[vmem_spec()],
        out_specs=vmem_spec(),
        out_shape=jax.ShapeDtypeStruct(parts.shape[1:], dtype),
        name="fold",
    )(parts)


def fold_chunks_kernel(parts_ref, out_ref, *, count, chunks):
    width = out_ref.shape[2]
    for j in range(chunks):
        cols = slice(j * width, (j + 1) * width)
        total = parts_ref[0, :, cols].astype(f32)
        for i in range(1, count):
            total = total + parts_ref[i, :, cols].astype(f32)
        out_ref[j] = total.astype(out_ref.dtype)


def fold_chunks(parts, chunks):
    count, rows, width = parts.shape
    return pl.pallas_call(
        functools.partial(fold_chunks_kernel, count=count, chunks=chunks),
        in_specs=[vmem_spec()],
        out_specs=vmem_spec(),
        out_shape=jax.ShapeDtypeStruct((chunks, rows, width // chunks), bf16),
        name="fold_chunks",
    )(parts)


def total_kernel(sums_ref, accum_ref, total_ref, square_ref, *, chunks, tokens):
    width = sums_ref.shape[2]
    square = jnp.zeros((accum_ref.shape[0], width), f32)
    for j in range(chunks):
        cols = slice(j * width, (j + 1) * width)
        total = accum_ref[:, cols] + sums_ref[j] * (1.0 / tokens)
        total_ref[:, cols] = total
        square = square + total * total
    square_ref[0, 0] = jnp.sum(square)


def total_of(sums, accum, tokens):
    return pl.pallas_call(
        functools.partial(total_kernel, chunks=sums.shape[0], tokens=tokens),
        in_specs=[vmem_spec()] * 2,
        out_specs=[vmem_spec(), pl.BlockSpec(memory_space=pltpu.SMEM)],
        out_shape=[
            jax.ShapeDtypeStruct(accum.shape, f32),
            jax.ShapeDtypeStruct((1, 1), f32),
        ],
        name="total_of",
    )(sums, accum)


def adam(total_grad, master, moment1, moment2, clip_factor):
    clipped = clip_factor * total_grad
    moment_one = beta_one * moment1 + (1.0 - beta_one) * clipped
    moment_two = beta_two * moment2 + (1.0 - beta_two) * clipped * clipped
    step = moment_one / bias_one / (jnp.sqrt(moment_two / bias_two) + epsilon) + decay_rate * master
    return step, master - learn_rate * step


def place_kernel(core_ref, order_ref, own_ref, other_ref, out_ref):
    side = pl.program_id(0)

    @pl.when(side == 0)
    def _():
        out_ref[...] = dot(order_ref[...], own_ref[...], ((1,), (0,))).astype(bf16)

    @pl.when(side == 1)
    def _():
        out_ref[...] = dot(order_ref[...], other_ref[...], ((1,), (0,))).astype(bf16)


def place(core, order, own, other, steps):
    slab, half = own.shape
    block = half // steps
    return pl.pallas_call(
        place_kernel,
        grid_spec=pltpu.PrefetchScalarGridSpec(
            num_scalar_prefetch=1,
            grid=(2, steps),
            in_specs=[
                pl.BlockSpec((slab, slab), lambda g, j, c: (0, 0)),
                pl.BlockSpec((slab, block), lambda g, j, c: (0, jnp.where(g == 0, j, steps - 1))),
                pl.BlockSpec((slab, block), lambda g, j, c: (0, jnp.where(g == 1, j, 0))),
            ],
            out_specs=pl.BlockSpec(
                (slab, block), lambda g, j, c: (0, jnp.where(g == 0, c[0], 1 - c[0]) * steps + j)
            ),
        ),
        out_shape=jax.ShapeDtypeStruct((slab, 2 * half), bf16),
        name="place",
    )(core, order, own, other)


def down(x, by):
    return lax.ppermute(x, "pipe", [(i, i - by) for i in range(by, 4)])


def swap(x, axis):
    return lax.ppermute(x, axis, [(0, 1), (1, 0)])


def local(top_grad, slab_inputs, weights, master, moment1, moment2, grad_accum, layer_counts):
    sizes = [lax.axis_size(axis) for axis in DP_AXES]
    n_y, n_z, n_x, n_core = sizes
    section = lax.axis_index("pipe").astype(jnp.int32)
    core = lax.axis_index("core").astype(jnp.int32)
    rows, width = top_grad.shape
    slab = slab_inputs.shape[2]
    span = 4 * slab
    half = width // 2
    tokens = rows * n_y * n_z * n_x * n_core
    slab_own, weight = slab_inputs[0], weights[0]
    shard = master.shape[1:]

    state = jnp.stack([master[0], moment1[0], moment2[0], grad_accum[0]])
    state = lax.all_gather(state, "z", axis=0, tiled=False)

    sent = lax.dynamic_slice(top_grad, (0, (1 - core) * half), (rows, half))
    other = swap(jnp.concatenate([sent, slab_own], axis=1), "core")
    slab_other = other[:, half:]

    w_sent = weight[:, 2 * slab : span]
    w_one = lax.ppermute(w_sent, "pipe", [(2, 1), (1, 0)])
    w_two = lax.ppermute(w_sent, "pipe", [(2, 0)])
    known = known_part(section[None], top_grad, weight, slab, span, 4)
    known_all = [known, down(known, 1), down(known, 2), down(known, 3)]
    top_head = top_grad[:, :span]
    head, section_grad = relay(
        section[None], top_head, known_all, [weight[:, :span], w_one, w_two], slab
    )
    head_other = swap(head, "core")

    here = jnp.arange(slab)
    source = (here % (n_y * n_z)) * n_x + here // (n_y * n_z)
    order = (jnp.arange(slab)[None, :] == source[:, None]).astype(bf16)
    product = slab_product(
        core[None], order, slab_own, slab_other, head, head_other, top_grad, other, 4
    )
    parts = lax.all_to_all(product, "x", split_axis=0, concat_axis=0, tiled=True)
    parts = fold(parts.reshape(n_x, slab // n_x, half), bf16)
    parts = lax.all_to_all(parts, "y", split_axis=0, concat_axis=0, tiled=True)
    parts = fold_chunks(parts.reshape(n_y, n_z, half), n_z)
    parts = lax.all_to_all(parts, "z", split_axis=0, concat_axis=0, tiled=True)
    sums = lax.all_gather(fold(parts, f32), "z", axis=0, tiled=False)

    state = state.transpose(1, 0, 2, 3).reshape(4, n_z, half)
    total_grad, square = total_of(sums, state[3], tokens)
    weighted = layer_counts.astype(f32)[section] * square[0, 0]
    weighted = lax.psum(weighted, "core")
    weighted = lax.psum(weighted, "x")
    square_norm = lax.psum(weighted, ("pipe", "y"))
    clip_factor = jnp.minimum(1.0, clip_norm / jnp.sqrt(square_norm))

    fresh = adam(total_grad, state[0], state[1], state[2], clip_factor)[1].astype(bf16)
    fresh = lax.all_gather(fresh, "y", axis=0, tiled=False)
    fresh = jnp.broadcast_to(fresh[None], (n_x, n_y, n_z, half))
    fresh = lax.all_to_all(fresh, "x", split_axis=0, concat_axis=0, tiled=True)
    fresh = fresh.reshape(slab, half)
    new_weights = place(core[None], order.T, fresh, swap(fresh, "core"), 4)

    own = lax.dynamic_slice(total_grad, (lax.axis_index("z"), 0), (1, half)).reshape(shard)
    adam_step, new_master = adam(own, master[0], moment1[0], moment2[0], clip_factor)
    return (new_weights[None], adam_step[None], new_master[None], section_grad[None])


def solution(mesh):
    devices = mesh.devices
    split = Mesh(devices.reshape((devices.shape[0],) + DP_SIZES), ("pipe",) + DP_AXES)
    return jax.shard_map(
        local,
        mesh=split,
        in_specs=(
            P(DP_AXES, None),
            P("pipe", DP_AXES, None),
            P("pipe", None, None),
            P("pipe", DP_AXES, None),
            P("pipe", DP_AXES, None),
            P("pipe", DP_AXES, None),
            P("pipe", DP_AXES, None),
            P(),
        ),
        out_specs=(
            P("pipe", None, None),
            P("pipe", DP_AXES, None),
            P("pipe", DP_AXES, None),
            P("pipe", DP_AXES, None),
        ),
        check_vma=False,
    )
```

```python
import functools
import jax
import jax.numpy as jnp
from jax import lax
from jax.experimental import pallas as pl
from jax.experimental.pallas import tpu as pltpu
from jax.sharding import Mesh, PartitionSpec as P

beta_one = 0.9
beta_two = 0.95
bias_one = 1.0 - 0.9**20
bias_two = 1.0 - 0.95**20
epsilon = 1e-08
decay_rate = 0.1
learn_rate = 0.0003
clip_norm = 1.0

bf16 = jnp.bfloat16
f32 = jnp.float32
DP_AXES = ("y", "z", "x", "core")
DP_SIZES = (2, 16, 4, 2)


def dot(a, b, dims):
    return lax.dot_general(a, b, (dims, ((), ())), preferred_element_type=f32)


def vmem_spec():
    return pl.BlockSpec(memory_space=pltpu.VMEM)


def known_kernel(section_ref, top_ref, weight_ref, out_ref, *, slab, span):
    step = pl.program_id(0)

    @pl.when(step == 0)
    def _():
        column = lax.broadcasted_iota(jnp.int32, top_ref.shape, 1)
        later = (column >= (section_ref[0] + 1) * slab) & (column < span)
        known = jnp.where(later, 0.0, top_ref[...].astype(f32)).astype(bf16)
        out_ref[...] = dot(known, weight_ref[...], ((1,), (1,)))

    @pl.when(step != 0)
    def _():
        out_ref[...] += dot(top_ref[...], weight_ref[...], ((1,), (1,)))


def known_part(section, top_grad, weight, slab, span, steps):
    rows, width = top_grad.shape
    block = width // steps
    return pl.pallas_call(
        functools.partial(known_kernel, slab=slab, span=span),
        grid_spec=pltpu.PrefetchScalarGridSpec(
            num_scalar_prefetch=1,
            grid=(steps,),
            in_specs=[
                pl.BlockSpec((rows, block), lambda i, s: (0, i)),
                pl.BlockSpec((slab, block), lambda i, s: (0, i)),
            ],
            out_specs=pl.BlockSpec((rows, slab), lambda i, s: (0, 0)),
        ),
        out_shape=jax.ShapeDtypeStruct((rows, slab), f32),
        name="known_part",
    )(section, top_grad, weight)


def relay_kernel(section_ref, top_ref, own_ref, one_ref, two_ref, three_ref, w_own_ref, w_one_ref, w_two_ref, head_ref, grad_ref, *, slab):
    section = section_ref[0]
    known = (own_ref, one_ref, two_ref, three_ref)
    for u in range(3, -1, -1):
        @pl.when(section <= u)
        def _(u=u):
            offset = u - section
            total = known[3][...]
            for k in (2, 1, 0):
                total = jnp.where(offset == k, known[k][...], total)
            for v in range(u + 1, 4):
                block = slice(v * slab, (v + 1) * slab)
                weight = w_own_ref[:, block].astype(f32)
                if v >= 2:
                    narrow = slice((v - 2) * slab, (v - 1) * slab)
                    weight = jnp.where(offset == 1, w_one_ref[:, narrow].astype(f32), weight)
                    weight = jnp.where(offset == 2, w_two_ref[:, narrow].astype(f32), weight)
                total = total + dot(head_ref[:, block], weight.astype(bf16), ((1,), (1,)))
            branch = total.astype(bf16)
            here = slice(u * slab, (u + 1) * slab)
            top = top_ref[:, here]
            placed = (top.astype(f32) + branch.astype(f32)).astype(bf16)
            head_ref[:, here] = jnp.where(offset == 0, top.astype(f32), placed.astype(f32)).astype(bf16)
            grad_ref[...] = branch

        @pl.when(section > u)
        def _(u=u):
            here = slice(u * slab, (u + 1) * slab)
            head_ref[:, here] = top_ref[:, here]


def relay(section, top_grad, known, weights, slab, span):
    rows = top_grad.shape[0]
    first = pl.BlockSpec((rows, span), lambda i: (0, 0))
    return pl.pallas_call(
        functools.partial(relay_kernel, slab=slab),
        grid=(1,),
        in_specs=[pl.BlockSpec(memory_space=pltpu.SMEM), first]
        + [pl.BlockSpec((rows, slab), lambda i: (0, 0))] * 4
        + [pl.BlockSpec((slab, span), lambda i: (0, 0))]
        + [pl.BlockSpec((slab, span // 2), lambda i: (0, 0))] * 2,
        out_specs=[first, pl.BlockSpec((rows, slab), lambda i: (0, 0))],
        out_shape=[
            jax.ShapeDtypeStruct((rows, span), bf16),
            jax.ShapeDtypeStruct((rows, slab), bf16),
        ],
        name="relay",
    )(section, top_grad, *known, *weights)


def product_kernel(core_ref, order_ref, slab_a_ref, slab_b_ref, head_a_ref, head_b_ref, top_ref, other_ref, out_ref, a_ref, b_ref, *, span):
    step = pl.program_id(0)

    @pl.when(step == 0)
    def _():
        a_ref[...] = dot(order_ref[...], slab_a_ref[...], ((1,), (1,))).astype(bf16)
        b_ref[...] = dot(order_ref[...], slab_b_ref[...], ((1,), (1,))).astype(bf16)

    out_ref[...] = (
        dot(a_ref[...], top_ref[...], ((1,), (0,))) + dot(b_ref[...], other_ref[...], ((1,), (0,)))
    ).astype(bf16)

    @pl.when((step == 0) & (core_ref[0] == 0))
    def _():
        out_ref[:, :span] = (
            dot(a_ref[...], head_a_ref[...], ((1,), (0,))) + dot(b_ref[...], head_b_ref[...], ((1,), (0,)))
        ).astype(bf16)


def slab_product(core, order, slab_a, slab_b, head_a, head_b, top_grad, other, steps):
    rows = top_grad.shape[0]
    slab = slab_a.shape[1]
    half = top_grad.shape[1] // 2
    span = head_a.shape[1]
    block = half // steps
    whole = lambda shape: pl.BlockSpec(shape, lambda i, c: (0, 0))
    return pl.pallas_call(
        functools.partial(product_kernel, span=span),
        grid_spec=pltpu.PrefetchScalarGridSpec(
            num_scalar_prefetch=1,
            grid=(steps,),
            in_specs=[
                whole((slab, slab)),
                whole((rows, slab)),
                whole((rows, slab)),
                whole((rows, span)),
                whole((rows, span)),
                pl.BlockSpec((rows, block), lambda i, c: (0, c[0] * steps + i)),
                pl.BlockSpec((rows, block), lambda i, c: (0, i)),
            ],
            out_specs=pl.BlockSpec((slab, block), lambda i, c: (0, i)),
            scratch_shapes=[pltpu.VMEM((slab, rows), bf16), pltpu.VMEM((slab, rows), bf16)],
        ),
        out_shape=jax.ShapeDtypeStruct((slab, half), bf16),
        name="slab_product",
    )(core, order, slab_a, slab_b, head_a, head_b, top_grad, other)


def fold_kernel(parts_ref, out_ref, *, count):
    total = parts_ref[0].astype(f32)
    for i in range(1, count):
        total = total + parts_ref[i].astype(f32)
    for i in range(count):
        out_ref[i] = total


def fold(parts):
    return pl.pallas_call(
        functools.partial(fold_kernel, count=parts.shape[0]),
        in_specs=[vmem_spec()],
        out_specs=vmem_spec(),
        out_shape=jax.ShapeDtypeStruct(parts.shape, f32),
        name="fold",
    )(parts)


def fold_chunks_kernel(parts_ref, out_ref, *, count, chunks):
    width = out_ref.shape[2]
    for j in range(chunks):
        cols = slice(j * width, (j + 1) * width)
        total = parts_ref[0, :, cols].astype(f32)
        for i in range(1, count):
            total = total + parts_ref[i, :, cols].astype(f32)
        out_ref[j] = total.astype(out_ref.dtype)


def fold_chunks(parts, chunks):
    count, rows, width = parts.shape
    return pl.pallas_call(
        functools.partial(fold_chunks_kernel, count=count, chunks=chunks),
        in_specs=[vmem_spec()],
        out_specs=vmem_spec(),
        out_shape=jax.ShapeDtypeStruct((chunks, rows, width // chunks), bf16),
        name="fold_chunks",
    )(parts)


def total_kernel(count_ref, sums_ref, accum_ref, total_ref, square_ref, *, chunks, tokens):
    width = sums_ref.shape[2]
    square = jnp.zeros((accum_ref.shape[0], width), f32)
    for j in range(chunks):
        cols = slice(j * width, (j + 1) * width)
        total = accum_ref[:, cols] + sums_ref[j] * (1.0 / tokens)
        total_ref[:, cols] = total
        square = square + total * total
    square_ref[...] = jnp.full(square_ref.shape, jnp.sum(square) * count_ref[0].astype(f32), f32)


def total_of(count, sums, accum, tokens, peers):
    return pl.pallas_call(
        functools.partial(total_kernel, chunks=sums.shape[0], tokens=tokens),
        in_specs=[pl.BlockSpec(memory_space=pltpu.SMEM)] + [vmem_spec()] * 2,
        out_specs=[vmem_spec()] * 2,
        out_shape=[
            jax.ShapeDtypeStruct(accum.shape, f32),
            jax.ShapeDtypeStruct((peers, 8, 128), f32),
        ],
        name="total_of",
    )(count, sums, accum)


def adam(total_grad, master, moment1, moment2, clip_factor):
    clipped = clip_factor * total_grad
    moment_one = beta_one * moment1 + (1.0 - beta_one) * clipped
    moment_two = beta_two * moment2 + (1.0 - beta_two) * clipped * clipped
    step = moment_one / bias_one / (jnp.sqrt(moment_two / bias_two) + epsilon) + decay_rate * master
    return step, master - learn_rate * step


def fresh_kernel(squares_ref, total_ref, state_ref, out_ref, factor_ref):
    square_norm = jnp.sum(squares_ref[...], axis=0)[:1]
    clip_factor = jnp.minimum(1.0, clip_norm / jnp.sqrt(square_norm))
    factor_ref[...] = jnp.broadcast_to(clip_factor, factor_ref.shape)
    lanes = factor_ref.shape[1]
    for j in range(total_ref.shape[1] // lanes):
        cols = slice(j * lanes, (j + 1) * lanes)
        out_ref[:, cols] = adam(
            total_ref[:, cols], state_ref[0, :, cols], state_ref[1, :, cols], state_ref[2, :, cols], clip_factor
        )[1].astype(bf16)


def fresh_weights(squares, total_grad, state):
    return pl.pallas_call(
        fresh_kernel,
        in_specs=[vmem_spec()] * 3,
        out_specs=[vmem_spec()] * 2,
        out_shape=[
            jax.ShapeDtypeStruct(total_grad.shape, bf16),
            jax.ShapeDtypeStruct((8, 128), f32),
        ],
        name="fresh_weights",
    )(squares, total_grad, state)


def place_kernel(side_ref, order_ref, half_ref, *refs):
    out_ref = refs[-1]
    out_ref[...] = dot(order_ref[...], half_ref[...], ((1,), (0,))).astype(bf16)


def place(side, order, values, steps, into=None):
    slab, half = values.shape
    block = half // steps
    rest = [] if into is None else [into]
    return pl.pallas_call(
        place_kernel,
        grid_spec=pltpu.PrefetchScalarGridSpec(
            num_scalar_prefetch=1,
            grid=(steps,),
            in_specs=[
                pl.BlockSpec((slab, slab), lambda j, c: (0, 0)),
                pl.BlockSpec((slab, block), lambda j, c: (0, j)),
            ]
            + [pl.BlockSpec(memory_space=pl.ANY)] * len(rest),
            out_specs=pl.BlockSpec((slab, block), lambda j, c: (0, c[0] * steps + j)),
        ),
        out_shape=jax.ShapeDtypeStruct((slab, 2 * half), bf16),
        input_output_aliases={3: 0} if rest else {},
        cost_estimate=pl.CostEstimate(
            flops=2 * slab * slab * half, bytes_accessed=4 * slab * half, transcendentals=0
        ),
        name="place",
    )(side, order, values, *rest)


def down(x, by):
    return lax.ppermute(x, "pipe", [(i, i - by) for i in range(by, 4)])


def swap(x, axis):
    return lax.ppermute(x, axis, [(0, 1), (1, 0)])


def local(top_grad, slab_inputs, weights, master, moment1, moment2, grad_accum, layer_counts):
    sizes = [lax.axis_size(axis) for axis in DP_AXES]
    n_y, n_z, n_x, n_core = sizes
    section = lax.axis_index("pipe").astype(jnp.int32)
    core = lax.axis_index("core").astype(jnp.int32)
    rows, width = top_grad.shape
    slab = slab_inputs.shape[2]
    span = 4 * slab
    half = width // 2
    tokens = rows * n_y * n_z * n_x * n_core
    slab_own, weight = slab_inputs[0], weights[0]
    shard = master.shape[1:]

    state = jnp.stack([master[0], moment1[0], moment2[0], grad_accum[0]])
    state = lax.all_gather(state, "z", axis=0, tiled=False)

    sent = lax.dynamic_slice(top_grad, (0, (1 - core) * half), (rows, half))
    other = swap(jnp.concatenate([sent, slab_own], axis=1), "core")
    slab_other = other[:, half:]

    w_sent = weight[:, 2 * slab : span]
    w_one = lax.ppermute(w_sent, "pipe", [(2, 1), (1, 0)])
    w_two = lax.ppermute(w_sent, "pipe", [(2, 0)])
    known = known_part(section[None], top_grad, weight, slab, span, 4)
    known_all = [known, down(known, 1), down(known, 2), down(known, 3)]
    head, section_grad = relay(
        section[None], top_grad, known_all, [weight, w_one, w_two], slab, span
    )
    head_other = swap(head, "core")

    here = jnp.arange(slab)
    source = here // (n_x * n_z) * (n_x * n_z) + here % n_z * n_x + here // n_z % n_x
    order = (here[None, :] == source[:, None]).astype(bf16)
    product = slab_product(
        core[None], order, slab_own, slab_other, head, head_other, top_grad, other, 4
    )
    parts = lax.all_to_all(product, ("y", "x"), split_axis=0, concat_axis=0, tiled=True)
    parts = fold_chunks(parts.reshape(n_y * n_x, n_z, half), n_z)
    parts = lax.all_to_all(parts, "z", split_axis=0, concat_axis=0, tiled=True)
    sums = lax.all_to_all(fold(parts), "z", split_axis=0, concat_axis=0, tiled=True)

    state = state.transpose(1, 0, 2, 3).reshape(4, n_z, half)
    group = ("pipe", "y", "x", "core")
    count = lax.dynamic_slice(layer_counts, (section,), (1,))
    total_grad, squares = total_of(count, sums, state[3], tokens, lax.axis_size(group))
    squares = lax.all_to_all(squares, group, split_axis=0, concat_axis=0, tiled=True)

    fresh, factor = fresh_weights(squares, total_grad, state[:3])
    fresh = lax.all_gather(fresh, "y", axis=0, tiled=False)
    fresh = jnp.broadcast_to(fresh[None], (n_x, n_y, n_z, half))
    fresh = lax.all_to_all(fresh, "x", split_axis=0, concat_axis=0, tiled=True)
    fresh = fresh.reshape(slab, half)
    source = here % n_x * (n_y * n_z) + here // n_x
    order = (here[None, :] == source[:, None]).astype(bf16)
    fresh_other = swap(fresh, "core")
    new_weights = place(core[None], order, fresh, 2)
    new_weights = place(1 - core[None], order, fresh_other, 2, new_weights)

    own = lax.dynamic_slice(total_grad, (lax.axis_index("z"), 0), (1, half)).reshape(shard)
    adam_step, new_master = adam(own, master[0], moment1[0], moment2[0], factor[0, 0])
    return (new_weights[None], adam_step[None], new_master[None], section_grad[None])


def solution(mesh):
    devices = mesh.devices
    split = Mesh(devices.reshape((devices.shape[0],) + DP_SIZES), ("pipe",) + DP_AXES)
    return jax.shard_map(
        local,
        mesh=split,
        in_specs=(
            P(DP_AXES, None),
            P("pipe", DP_AXES, None),
            P("pipe", None, None),
            P("pipe", DP_AXES, None),
            P("pipe", DP_AXES, None),
            P("pipe", DP_AXES, None),
            P("pipe", DP_AXES, None),
            P(),
        ),
        out_specs=(
            P("pipe", None, None),
            P("pipe", DP_AXES, None),
            P("pipe", DP_AXES, None),
            P("pipe", DP_AXES, None),
        ),
        check_vma=False,
    )
```

```python
import functools
import jax
import jax.numpy as jnp
from jax import lax
from jax.experimental import pallas as pl
from jax.experimental.pallas import tpu as pltpu
from jax.sharding import Mesh, PartitionSpec as P

beta_one = 0.9
beta_two = 0.95
bias_one = 1.0 - 0.9**20
bias_two = 1.0 - 0.95**20
epsilon = 1e-08
decay_rate = 0.1
learn_rate = 0.0003
clip_norm = 1.0

bf16 = jnp.bfloat16
f32 = jnp.float32
DP_AXES = ("y", "z", "x", "core")
DP_SIZES = (2, 16, 4, 2)


def dot(a, b, dims):
    return lax.dot_general(a, b, (dims, ((), ())), preferred_element_type=f32)


def vmem_spec():
    return pl.BlockSpec(memory_space=pltpu.VMEM)


def known_kernel(section_ref, top_ref, weight_ref, out_ref, *, slab, span):
    step = pl.program_id(0)

    @pl.when(step == 0)
    def _():
        column = lax.broadcasted_iota(jnp.int32, top_ref.shape, 1)
        later = (column >= (section_ref[0] + 1) * slab) & (column < span)
        known = jnp.where(later, 0.0, top_ref[...].astype(f32)).astype(bf16)
        out_ref[...] = dot(known, weight_ref[...], ((1,), (1,)))

    @pl.when(step != 0)
    def _():
        out_ref[...] += dot(top_ref[...], weight_ref[...], ((1,), (1,)))


def known_part(section, top_grad, weight, slab, span, steps):
    rows, width = top_grad.shape
    block = width // steps
    return pl.pallas_call(
        functools.partial(known_kernel, slab=slab, span=span),
        grid_spec=pltpu.PrefetchScalarGridSpec(
            num_scalar_prefetch=1,
            grid=(steps,),
            in_specs=[
                pl.BlockSpec((rows, block), lambda i, s: (0, i)),
                pl.BlockSpec((slab, block), lambda i, s: (0, i)),
            ],
            out_specs=pl.BlockSpec((rows, slab), lambda i, s: (0, 0)),
        ),
        out_shape=jax.ShapeDtypeStruct((rows, slab), f32),
        name="known_part",
    )(section, top_grad, weight)


def relay_kernel(section_ref, top_ref, own_ref, one_ref, two_ref, three_ref, w_own_ref, w_one_ref, w_two_ref, head_ref, grad_ref, *, slab):
    section = section_ref[0]
    known = (own_ref, one_ref, two_ref, three_ref)
    for u in range(3, -1, -1):
        @pl.when(section <= u)
        def _(u=u):
            offset = u - section
            total = known[3][...]
            for k in (2, 1, 0):
                total = jnp.where(offset == k, known[k][...], total)
            for v in range(u + 1, 4):
                block = slice(v * slab, (v + 1) * slab)
                weight = w_own_ref[:, block].astype(f32)
                if v >= 2:
                    narrow = slice((v - 2) * slab, (v - 1) * slab)
                    weight = jnp.where(offset == 1, w_one_ref[:, narrow].astype(f32), weight)
                    weight = jnp.where(offset == 2, w_two_ref[:, narrow].astype(f32), weight)
                total = total + dot(head_ref[:, block], weight.astype(bf16), ((1,), (1,)))
            branch = total.astype(bf16)
            here = slice(u * slab, (u + 1) * slab)
            top = top_ref[:, here]
            placed = (top.astype(f32) + branch.astype(f32)).astype(bf16)
            head_ref[:, here] = jnp.where(offset == 0, top.astype(f32), placed.astype(f32)).astype(bf16)
            grad_ref[...] = branch

        @pl.when(section > u)
        def _(u=u):
            here = slice(u * slab, (u + 1) * slab)
            head_ref[:, here] = top_ref[:, here]


def relay(section, top_grad, known, weights, slab, span):
    rows = top_grad.shape[0]
    first = pl.BlockSpec((rows, span), lambda i: (0, 0))
    return pl.pallas_call(
        functools.partial(relay_kernel, slab=slab),
        grid=(1,),
        in_specs=[pl.BlockSpec(memory_space=pltpu.SMEM), first]
        + [pl.BlockSpec((rows, slab), lambda i: (0, 0))] * 4
        + [pl.BlockSpec((slab, span), lambda i: (0, 0))]
        + [pl.BlockSpec((slab, span // 2), lambda i: (0, 0))] * 2,
        out_specs=[first, pl.BlockSpec((rows, slab), lambda i: (0, 0))],
        out_shape=[
            jax.ShapeDtypeStruct((rows, span), bf16),
            jax.ShapeDtypeStruct((rows, slab), bf16),
        ],
        name="relay",
    )(section, top_grad, *known, *weights)


def turn_kernel(order_ref, a_in_ref, b_in_ref, a_ref, b_ref):
    a_ref[...] = dot(order_ref[...], a_in_ref[...], ((1,), (1,))).astype(bf16)
    b_ref[...] = dot(order_ref[...], b_in_ref[...], ((1,), (1,))).astype(bf16)


def tail_kernel(core_ref, order_ref, slab_a_ref, slab_b_ref, top_ref, other_ref, out_ref, a_ref, b_ref):
    @pl.when(pl.program_id(0) == 0)
    def _():
        turn_kernel(order_ref, slab_a_ref, slab_b_ref, a_ref, b_ref)

    out_ref[...] = (
        dot(a_ref[...], top_ref[...], ((1,), (0,))) + dot(b_ref[...], other_ref[...], ((1,), (0,)))
    ).astype(bf16)


def tail_product(core, order, slab_a, top_grad, other, span):
    rows, width = top_grad.shape
    slab = slab_a.shape[1]
    half = width // 2
    blocks = half // span
    whole = pl.BlockSpec((rows, slab), lambda i, c: (0, 0))
    turned = pl.BlockSpec((slab, rows), lambda i, c: (0, 0))
    return pl.pallas_call(
        tail_kernel,
        grid_spec=pltpu.PrefetchScalarGridSpec(
            num_scalar_prefetch=1,
            grid=(blocks - 1,),
            in_specs=[
                turned,
                whole,
                pl.BlockSpec((rows, slab), lambda i, c: (0, half // slab)),
                pl.BlockSpec((rows, span), lambda i, c: (0, c[0] * blocks + i + 1)),
                pl.BlockSpec((rows, span), lambda i, c: (0, i + 1)),
            ],
            out_specs=[pl.BlockSpec((slab, span), lambda i, c: (0, i)), turned, turned],
        ),
        out_shape=[
            jax.ShapeDtypeStruct((slab, half - span), bf16),
            jax.ShapeDtypeStruct((slab, rows), bf16),
            jax.ShapeDtypeStruct((slab, rows), bf16),
        ],
        name="tail_product",
    )(core, order, slab_a, other, top_grad, other)


def head_kernel(core_ref, a_ref, b_ref, head_a_ref, head_b_ref, top_ref, other_ref, out_ref):
    @pl.when(core_ref[0] == 0)
    def _():
        out_ref[...] = (
            dot(a_ref[...], head_a_ref[...], ((1,), (0,))) + dot(b_ref[...], head_b_ref[...], ((1,), (0,)))
        ).astype(bf16)

    @pl.when(core_ref[0] != 0)
    def _():
        out_ref[...] = (
            dot(a_ref[...], top_ref[...], ((1,), (0,))) + dot(b_ref[...], other_ref[...], ((1,), (0,)))
        ).astype(bf16)


def head_product(core, a, b, head_a, head_b, top_grad, other):
    rows, span = head_a.shape
    slab = a.shape[0]
    blocks = top_grad.shape[1] // 2 // span
    turned = pl.BlockSpec((slab, rows), lambda i, c: (0, 0))
    first = pl.BlockSpec((rows, span), lambda i, c: (0, 0))
    return pl.pallas_call(
        head_kernel,
        grid_spec=pltpu.PrefetchScalarGridSpec(
            num_scalar_prefetch=1,
            grid=(1,),
            in_specs=[turned, turned, first, first, pl.BlockSpec((rows, span), lambda i, c: (0, c[0] * blocks)), first],
            out_specs=pl.BlockSpec((slab, span), lambda i, c: (0, 0)),
        ),
        out_shape=jax.ShapeDtypeStruct((slab, span), bf16),
        name="head_product",
    )(core, a, b, head_a, head_b, top_grad, other)


def fold_kernel(parts_ref, out_ref, *, count):
    total = parts_ref[0].astype(f32)
    for i in range(1, count):
        total = total + parts_ref[i].astype(f32)
    for i in range(count):
        out_ref[i] = total


def fold(parts):
    return pl.pallas_call(
        functools.partial(fold_kernel, count=parts.shape[0]),
        in_specs=[vmem_spec()],
        out_specs=vmem_spec(),
        out_shape=jax.ShapeDtypeStruct(parts.shape, f32),
        name="fold",
    )(parts)


def fold_chunks_kernel(row_ref, accum_ref, head_ref, tail_ref, out_ref, *, tokens):
    count, rows, span = head_ref.shape
    chunks, _, width = out_ref.shape
    own = lax.broadcasted_iota(jnp.int32, (rows, width), 0) == row_ref[0]
    for j in range(chunks):
        at = j * width
        ref, start = (head_ref, at) if at < span else (tail_ref, at - span)
        cols = slice(start, start + width)
        total = jnp.where(own, accum_ref[:, at : at + width] * tokens, 0.0)
        for i in range(count):
            total = total + ref[i, :, cols].astype(f32)
        out_ref[j] = total.astype(bf16)


def fold_chunks(row, accum, head, tail, chunks, tokens):
    rows = head.shape[1]
    width = accum.shape[1]
    return pl.pallas_call(
        functools.partial(fold_chunks_kernel, tokens=float(tokens)),
        in_specs=[pl.BlockSpec(memory_space=pltpu.SMEM)] + [vmem_spec()] * 3,
        out_specs=vmem_spec(),
        out_shape=jax.ShapeDtypeStruct((chunks, rows, width // chunks), bf16),
        name="fold_chunks",
    )(row, accum, head, tail)


def total_kernel(count_ref, sums_ref, total_ref, square_ref, *, chunks, tokens):
    rows, width = sums_ref.shape[1:]
    square = jnp.zeros((rows, width), f32)
    for j in range(chunks):
        cols = slice(j * width, (j + 1) * width)
        total = sums_ref[j] * (1.0 / tokens)
        total_ref[:, cols] = total
        square = square + total * total
    square_ref[...] = jnp.full(square_ref.shape, jnp.sum(square) * count_ref[0].astype(f32), f32)


def total_of(count, sums, tokens, peers):
    chunks, rows, width = sums.shape
    return pl.pallas_call(
        functools.partial(total_kernel, chunks=sums.shape[0], tokens=tokens),
        in_specs=[pl.BlockSpec(memory_space=pltpu.SMEM), vmem_spec()],
        out_specs=[vmem_spec()] * 2,
        out_shape=[
            jax.ShapeDtypeStruct((rows, chunks * width), f32),
            jax.ShapeDtypeStruct((peers, 8, 128), f32),
        ],
        name="total_of",
    )(count, sums)


def adam(total_grad, master, moment1, moment2, clip_factor):
    clipped = clip_factor * total_grad
    moment_one = beta_one * moment1 + (1.0 - beta_one) * clipped
    moment_two = beta_two * moment2 + (1.0 - beta_two) * clipped * clipped
    step = moment_one / bias_one / (jnp.sqrt(moment_two / bias_two) + epsilon) + decay_rate * master
    return step, master - learn_rate * step


def fresh_kernel(squares_ref, total_ref, state_ref, out_ref, factor_ref):
    square_norm = jnp.sum(squares_ref[...], axis=0)[:1]
    clip_factor = jnp.minimum(1.0, clip_norm / jnp.sqrt(square_norm))
    factor_ref[...] = jnp.broadcast_to(clip_factor, factor_ref.shape)
    lanes = factor_ref.shape[1]
    for j in range(total_ref.shape[1] // lanes):
        cols = slice(j * lanes, (j + 1) * lanes)
        out_ref[:, cols] = adam(
            total_ref[:, cols], state_ref[0, :, cols], state_ref[1, :, cols], state_ref[2, :, cols], clip_factor
        )[1].astype(bf16)


def fresh_weights(squares, total_grad, state):
    return pl.pallas_call(
        fresh_kernel,
        in_specs=[vmem_spec()] * 3,
        out_specs=[vmem_spec()] * 2,
        out_shape=[
            jax.ShapeDtypeStruct(total_grad.shape, bf16),
            jax.ShapeDtypeStruct((8, 128), f32),
        ],
        name="fresh_weights",
    )(squares, total_grad, state)


def place_kernel(side_ref, order_ref, half_ref, *refs):
    out_ref = refs[-1]
    out_ref[...] = dot(order_ref[...], half_ref[...], ((1,), (0,))).astype(bf16)


def place(side, order, values, steps, into=None):
    slab, half = values.shape
    block = half // steps
    rest = [] if into is None else [into]
    return pl.pallas_call(
        place_kernel,
        grid_spec=pltpu.PrefetchScalarGridSpec(
            num_scalar_prefetch=1,
            grid=(steps,),
            in_specs=[
                pl.BlockSpec((slab, slab), lambda j, c: (0, 0)),
                pl.BlockSpec((slab, block), lambda j, c: (0, j)),
            ]
            + [pl.BlockSpec(memory_space=pl.ANY)] * len(rest),
            out_specs=pl.BlockSpec((slab, block), lambda j, c: (0, c[0] * steps + j)),
        ),
        out_shape=jax.ShapeDtypeStruct((slab, 2 * half), bf16),
        input_output_aliases={3: 0} if rest else {},
        cost_estimate=pl.CostEstimate(
            flops=2 * slab * slab * half, bytes_accessed=4 * slab * half, transcendentals=0
        ),
        name="place",
    )(side, order, values, *rest)


def down(x, by):
    return lax.ppermute(x, "pipe", [(i, i - by) for i in range(by, 4)])


def swap(x, axis):
    return lax.ppermute(x, axis, [(0, 1), (1, 0)])


def local(top_grad, slab_inputs, weights, master, moment1, moment2, grad_accum, layer_counts):
    sizes = [lax.axis_size(axis) for axis in DP_AXES]
    n_y, n_z, n_x, n_core = sizes
    section = lax.axis_index("pipe").astype(jnp.int32)
    core = lax.axis_index("core").astype(jnp.int32)
    rows, width = top_grad.shape
    slab = slab_inputs.shape[2]
    span = 4 * slab
    half = width // 2
    tokens = rows * n_y * n_z * n_x * n_core
    slab_own, weight = slab_inputs[0], weights[0]
    shard = master.shape[1:]

    state = jnp.stack([master[0], moment1[0], moment2[0], grad_accum[0]])
    state = lax.all_gather(state, "z", axis=0, tiled=False)

    sent = lax.dynamic_slice(top_grad, (0, (1 - core) * half), (rows, half))
    other = swap(jnp.concatenate([sent, slab_own], axis=1), "core")

    known = known_part(section[None], top_grad, weight, slab, span, 4)
    known_all = [known, down(known, 1), down(known, 2), down(known, 3)]
    w_sent = lax.optimization_barrier((weight, known))[0][:, 2 * slab : span]
    w_one = lax.ppermute(w_sent, "pipe", [(2, 1), (1, 0)])
    w_two = lax.ppermute(w_sent, "pipe", [(2, 0)])

    here = jnp.arange(slab)
    source = here // (n_x * n_z) * (n_x * n_z) + here % n_z * n_x + here // n_z % n_x
    order = (here[None, :] == source[:, None]).astype(bf16)
    other, known = lax.optimization_barrier((other, known))
    tail, slab_a, slab_b = tail_product(core[None], order, slab_own, top_grad, other, span)
    tail = lax.all_to_all(tail, ("y", "x"), split_axis=0, concat_axis=0, tiled=True)

    head, section_grad = relay(
        section[None], top_grad, known_all, [weight, w_one, w_two], slab, span
    )
    head_other = swap(head, "core")
    ahead = head_product(core[None], slab_a, slab_b, head, head_other, top_grad, other)
    ahead, tail = lax.optimization_barrier((ahead, tail))
    ahead = lax.all_to_all(ahead, ("y", "x"), split_axis=0, concat_axis=0, tiled=True)

    row = lax.axis_index("z").astype(jnp.int32)
    parts = fold_chunks(
        row[None],
        grad_accum[0].reshape(1, half),
        ahead.reshape(n_y * n_x, n_z, span),
        tail.reshape(n_y * n_x, n_z, half - span),
        n_z,
        tokens,
    )
    parts = lax.all_to_all(parts, "z", split_axis=0, concat_axis=0, tiled=True)
    sums = lax.all_to_all(fold(parts), "z", split_axis=0, concat_axis=0, tiled=True)

    group = ("pipe", "y", "x", "core")
    count = lax.dynamic_slice(layer_counts, (section,), (1,))
    total_grad, squares = total_of(count, sums, tokens, lax.axis_size(group))
    squares, state = lax.optimization_barrier((squares, state))
    squares = lax.all_to_all(squares, group, split_axis=0, concat_axis=0, tiled=True)

    state = state.transpose(1, 0, 2, 3).reshape(4, n_z, half)
    fresh, factor = fresh_weights(squares, total_grad, state[:3])
    fresh = lax.all_gather(fresh, "y", axis=0, tiled=False)
    fresh = jnp.broadcast_to(fresh[None], (n_x, n_y, n_z, half))
    fresh = lax.all_to_all(fresh, "x", split_axis=0, concat_axis=0, tiled=True)
    fresh = fresh.reshape(slab, half)
    source = here % n_x * (n_y * n_z) + here // n_x
    order = (here[None, :] == source[:, None]).astype(bf16)
    fresh_other = swap(fresh, "core")
    new_weights = place(core[None], order, fresh, 2)
    new_weights = place(1 - core[None], order, fresh_other, 2, new_weights)

    own = lax.dynamic_slice(total_grad, (row, 0), (1, half)).reshape(shard)
    adam_step, new_master = adam(own, master[0], moment1[0], moment2[0], factor[0, 0])
    return (new_weights[None], adam_step[None], new_master[None], section_grad[None])


def solution(mesh):
    devices = mesh.devices
    split = Mesh(devices.reshape((devices.shape[0],) + DP_SIZES), ("pipe",) + DP_AXES)
    return jax.shard_map(
        local,
        mesh=split,
        in_specs=(
            P(DP_AXES, None),
            P("pipe", DP_AXES, None),
            P("pipe", None, None),
            P("pipe", DP_AXES, None),
            P("pipe", DP_AXES, None),
            P("pipe", DP_AXES, None),
            P("pipe", DP_AXES, None),
            P(),
        ),
        out_specs=(
            P("pipe", None, None),
            P("pipe", DP_AXES, None),
            P("pipe", DP_AXES, None),
            P("pipe", DP_AXES, None),
        ),
        check_vma=False,
    )
```

```python
import functools
import jax
import jax.numpy as jnp
from jax import lax
from jax.experimental import pallas as pl
from jax.experimental.pallas import tpu as pltpu
from jax.sharding import Mesh, PartitionSpec as P

beta_one = 0.9
beta_two = 0.95
bias_one = 1.0 - 0.9**20
bias_two = 1.0 - 0.95**20
epsilon = 1e-08
decay_rate = 0.1
learn_rate = 0.0003
clip_norm = 1.0

bf16 = jnp.bfloat16
f32 = jnp.float32
VMEM_BYTES = 16 * 2**20
DP_AXES = ("y", "z", "x", "core")
DP_SIZES = (2, 16, 4, 2)


def dot(a, b, dims):
    return lax.dot_general(a, b, (dims, ((), ())), preferred_element_type=f32)


def vmem_spec():
    return pl.BlockSpec(memory_space=pltpu.VMEM)


def known_kernel(section_ref, top_ref, weight_ref, out_ref, *, slab, span):
    step = pl.program_id(0)

    @pl.when(step == 0)
    def _():
        column = lax.broadcasted_iota(jnp.int32, top_ref.shape, 1)
        later = (column >= (section_ref[0] + 1) * slab) & (column < span)
        known = jnp.where(later, 0.0, top_ref[...].astype(f32)).astype(bf16)
        out_ref[...] = dot(known, weight_ref[...], ((1,), (1,)))

    @pl.when(step != 0)
    def _():
        out_ref[...] += dot(top_ref[...], weight_ref[...], ((1,), (1,)))


def known_part(section, top_grad, weight, slab, span, steps):
    rows, width = top_grad.shape
    block = width // steps
    return pl.pallas_call(
        functools.partial(known_kernel, slab=slab, span=span),
        grid_spec=pltpu.PrefetchScalarGridSpec(
            num_scalar_prefetch=1,
            grid=(steps,),
            in_specs=[
                pl.BlockSpec((rows, block), lambda i, s: (0, i)),
                pl.BlockSpec((slab, block), lambda i, s: (0, i)),
            ],
            out_specs=pl.BlockSpec((rows, slab), lambda i, s: (0, 0)),
        ),
        out_shape=jax.ShapeDtypeStruct((rows, slab), f32),
        compiler_params=pltpu.CompilerParams(vmem_limit_bytes=56 * 2**20),
        name="known_part",
    )(section, top_grad, weight)


def relay_kernel(section_ref, top_ref, own_ref, one_ref, two_ref, three_ref, w_own_ref, w_one_ref, w_two_ref, head_ref, grad_ref, *, slab):
    section = section_ref[0]
    known = (own_ref, one_ref, two_ref, three_ref)
    for u in range(3, -1, -1):
        @pl.when(section <= u)
        def _(u=u):
            offset = u - section
            total = known[3][...]
            for k in (2, 1, 0):
                total = jnp.where(offset == k, known[k][...], total)
            for v in range(u + 1, 4):
                block = slice(v * slab, (v + 1) * slab)
                weight = w_own_ref[:, block].astype(f32)
                if v >= 2:
                    narrow = slice((v - 2) * slab, (v - 1) * slab)
                    weight = jnp.where(offset == 1, w_one_ref[:, narrow].astype(f32), weight)
                    weight = jnp.where(offset == 2, w_two_ref[:, narrow].astype(f32), weight)
                total = total + dot(head_ref[:, block], weight.astype(bf16), ((1,), (1,)))
            branch = total.astype(bf16)
            here = slice(u * slab, (u + 1) * slab)
            top = top_ref[:, here]
            placed = (top.astype(f32) + branch.astype(f32)).astype(bf16)
            head_ref[:, here] = jnp.where(offset == 0, top.astype(f32), placed.astype(f32)).astype(bf16)
            grad_ref[...] = branch

        @pl.when(section > u)
        def _(u=u):
            here = slice(u * slab, (u + 1) * slab)
            head_ref[:, here] = top_ref[:, here]


def relay(section, top_grad, known, weights, slab, span):
    rows = top_grad.shape[0]
    first = pl.BlockSpec((rows, span), lambda i: (0, 0))
    return pl.pallas_call(
        functools.partial(relay_kernel, slab=slab),
        grid=(1,),
        in_specs=[pl.BlockSpec(memory_space=pltpu.SMEM), first]
        + [pl.BlockSpec((rows, slab), lambda i: (0, 0))] * 4
        + [pl.BlockSpec((slab, span), lambda i: (0, 0))]
        + [pl.BlockSpec((slab, span // 2), lambda i: (0, 0))] * 2,
        out_specs=[first, pl.BlockSpec((rows, slab), lambda i: (0, 0))],
        out_shape=[
            jax.ShapeDtypeStruct((rows, span), bf16),
            jax.ShapeDtypeStruct((rows, slab), bf16),
        ],
        compiler_params=pltpu.CompilerParams(vmem_limit_bytes=VMEM_BYTES),
        name="relay",
    )(section, top_grad, *known, *weights)


def turn_kernel(order_ref, a_in_ref, b_in_ref, a_ref, b_ref):
    a_ref[...] = dot(order_ref[...], a_in_ref[...], ((1,), (1,))).astype(bf16)
    b_ref[...] = dot(order_ref[...], b_in_ref[...], ((1,), (1,))).astype(bf16)


def tail_kernel(core_ref, order_ref, slab_a_ref, slab_b_ref, top_ref, other_ref, out_ref, a_ref, b_ref):
    @pl.when(pl.program_id(0) == 0)
    def _():
        turn_kernel(order_ref, slab_a_ref, slab_b_ref, a_ref, b_ref)

    out_ref[...] = (
        dot(a_ref[...], top_ref[...], ((1,), (0,))) + dot(b_ref[...], other_ref[...], ((1,), (0,)))
    ).astype(bf16)


def tail_product(core, order, slab_a, top_grad, other, span):
    rows, width = top_grad.shape
    slab = slab_a.shape[1]
    half = width // 2
    blocks = half // span
    whole = pl.BlockSpec((rows, slab), lambda i, c: (0, 0))
    turned = pl.BlockSpec((slab, rows), lambda i, c: (0, 0))
    return pl.pallas_call(
        tail_kernel,
        grid_spec=pltpu.PrefetchScalarGridSpec(
            num_scalar_prefetch=1,
            grid=(blocks - 1,),
            in_specs=[
                turned,
                whole,
                pl.BlockSpec((rows, slab), lambda i, c: (0, half // slab)),
                pl.BlockSpec((rows, span), lambda i, c: (0, c[0] * blocks + i + 1)),
                pl.BlockSpec((rows, span), lambda i, c: (0, i + 1)),
            ],
            out_specs=[pl.BlockSpec((slab, span), lambda i, c: (0, i + 1)), turned, turned],
        ),
        out_shape=[
            jax.ShapeDtypeStruct((slab, half), bf16),
            jax.ShapeDtypeStruct((slab, rows), bf16),
            jax.ShapeDtypeStruct((slab, rows), bf16),
        ],
        compiler_params=pltpu.CompilerParams(vmem_limit_bytes=VMEM_BYTES),
        name="tail_product",
    )(core, order, slab_a, other, top_grad, other)


def head_kernel(core_ref, a_ref, b_ref, head_a_ref, head_b_ref, top_ref, other_ref, tail_ref, out_ref):
    @pl.when(core_ref[0] == 0)
    def _():
        out_ref[...] = (
            dot(a_ref[...], head_a_ref[...], ((1,), (0,))) + dot(b_ref[...], head_b_ref[...], ((1,), (0,)))
        ).astype(bf16)

    @pl.when(core_ref[0] != 0)
    def _():
        out_ref[...] = (
            dot(a_ref[...], top_ref[...], ((1,), (0,))) + dot(b_ref[...], other_ref[...], ((1,), (0,)))
        ).astype(bf16)


def head_product(core, a, b, head_a, head_b, top_grad, other, tail):
    rows, span = head_a.shape
    slab = a.shape[0]
    blocks = top_grad.shape[1] // 2 // span
    turned = pl.BlockSpec((slab, rows), lambda i, c: (0, 0))
    first = pl.BlockSpec((rows, span), lambda i, c: (0, 0))
    return pl.pallas_call(
        head_kernel,
        grid_spec=pltpu.PrefetchScalarGridSpec(
            num_scalar_prefetch=1,
            grid=(1,),
            in_specs=[turned, turned, first, first, pl.BlockSpec((rows, span), lambda i, c: (0, c[0] * blocks)), first]
            + [pl.BlockSpec(memory_space=pl.ANY)],
            out_specs=pl.BlockSpec((slab, span), lambda i, c: (0, 0)),
        ),
        out_shape=jax.ShapeDtypeStruct(tail.shape, bf16),
        input_output_aliases={7: 0},
        compiler_params=pltpu.CompilerParams(vmem_limit_bytes=VMEM_BYTES),
        name="head_product",
    )(core, a, b, head_a, head_b, top_grad, other, tail)


def fold_kernel(parts_ref, out_ref, *, count):
    total = parts_ref[0].astype(f32)
    for i in range(1, count):
        total = total + parts_ref[i].astype(f32)
    for i in range(count):
        out_ref[i] = total


def fold(parts):
    return pl.pallas_call(
        functools.partial(fold_kernel, count=parts.shape[0]),
        in_specs=[vmem_spec()],
        out_specs=vmem_spec(),
        out_shape=jax.ShapeDtypeStruct(parts.shape, f32),
        compiler_params=pltpu.CompilerParams(vmem_limit_bytes=VMEM_BYTES),
        name="fold",
    )(parts)


def fold_chunks_kernel(row_ref, accum_ref, parts_ref, out_ref, *, tokens):
    count, rows, _ = parts_ref.shape
    chunks, _, width = out_ref.shape
    own = lax.broadcasted_iota(jnp.int32, (rows, width), 0) == row_ref[0]
    for j in range(chunks):
        cols = slice(j * width, (j + 1) * width)
        total = jnp.where(own, accum_ref[:, cols] * tokens, 0.0)
        for i in range(count):
            total = total + parts_ref[i, :, cols].astype(f32)
        out_ref[j] = total.astype(bf16)


def fold_chunks(row, accum, parts, chunks, tokens):
    _, rows, width = parts.shape
    return pl.pallas_call(
        functools.partial(fold_chunks_kernel, tokens=float(tokens)),
        in_specs=[pl.BlockSpec(memory_space=pltpu.SMEM)] + [vmem_spec()] * 2,
        out_specs=vmem_spec(),
        out_shape=jax.ShapeDtypeStruct((chunks, rows, width // chunks), bf16),
        compiler_params=pltpu.CompilerParams(vmem_limit_bytes=VMEM_BYTES),
        name="fold_chunks",
    )(row, accum, parts)


def total_kernel(count_ref, sums_ref, total_ref, square_ref, *, chunks, tokens):
    rows, width = sums_ref.shape[1:]
    square = jnp.zeros((rows, width), f32)
    for j in range(chunks):
        cols = slice(j * width, (j + 1) * width)
        total = sums_ref[j] * (1.0 / tokens)
        total_ref[:, cols] = total
        square = square + total * total
    square_ref[...] = jnp.full(square_ref.shape, jnp.sum(square) * count_ref[0].astype(f32), f32)


def total_of(count, sums, tokens, peers):
    chunks, rows, width = sums.shape
    return pl.pallas_call(
        functools.partial(total_kernel, chunks=sums.shape[0], tokens=tokens),
        in_specs=[pl.BlockSpec(memory_space=pltpu.SMEM), vmem_spec()],
        out_specs=[vmem_spec()] * 2,
        out_shape=[
            jax.ShapeDtypeStruct((rows, chunks * width), f32),
            jax.ShapeDtypeStruct((peers, 8, 128), f32),
        ],
        compiler_params=pltpu.CompilerParams(vmem_limit_bytes=VMEM_BYTES),
        name="total_of",
    )(count, sums)


def adam(total_grad, master, moment1, moment2, clip_factor):
    clipped = clip_factor * total_grad
    moment_one = beta_one * moment1 + (1.0 - beta_one) * clipped
    moment_two = beta_two * moment2 + (1.0 - beta_two) * clipped * clipped
    step = moment_one / bias_one / (jnp.sqrt(moment_two / bias_two) + epsilon) + decay_rate * master
    return step, master - learn_rate * step


def fresh_kernel(squares_ref, total_ref, state_ref, out_ref, factor_ref):
    square_norm = jnp.sum(squares_ref[...], axis=0)[:1]
    clip_factor = jnp.minimum(1.0, clip_norm / jnp.sqrt(square_norm))
    factor_ref[...] = jnp.broadcast_to(clip_factor, factor_ref.shape)
    lanes = factor_ref.shape[1]
    for j in range(total_ref.shape[1] // lanes):
        cols = slice(j * lanes, (j + 1) * lanes)
        out_ref[:, cols] = adam(
            total_ref[:, cols], state_ref[0, :, cols], state_ref[1, :, cols], state_ref[2, :, cols], clip_factor
        )[1].astype(bf16)


def fresh_weights(squares, total_grad, state):
    return pl.pallas_call(
        fresh_kernel,
        in_specs=[vmem_spec()] * 3,
        out_specs=[vmem_spec()] * 2,
        out_shape=[
            jax.ShapeDtypeStruct(total_grad.shape, bf16),
            jax.ShapeDtypeStruct((8, 128), f32),
        ],
        compiler_params=pltpu.CompilerParams(vmem_limit_bytes=VMEM_BYTES),
        name="fresh_weights",
    )(squares, total_grad, state)


def place_kernel(side_ref, order_ref, half_ref, *refs):
    out_ref = refs[-1]
    out_ref[...] = dot(order_ref[...], half_ref[...], ((1,), (0,))).astype(bf16)


def place(side, order, values, steps, into=None):
    slab, half = values.shape
    block = half // steps
    rest = [] if into is None else [into]
    return pl.pallas_call(
        place_kernel,
        grid_spec=pltpu.PrefetchScalarGridSpec(
            num_scalar_prefetch=1,
            grid=(steps,),
            in_specs=[
                pl.BlockSpec((slab, slab), lambda j, c: (0, 0)),
                pl.BlockSpec((slab, block), lambda j, c: (0, j)),
            ]
            + [pl.BlockSpec(memory_space=pl.ANY)] * len(rest),
            out_specs=pl.BlockSpec((slab, block), lambda j, c: (0, c[0] * steps + j)),
        ),
        out_shape=jax.ShapeDtypeStruct((slab, 2 * half), bf16),
        input_output_aliases={3: 0} if rest else {},
        cost_estimate=pl.CostEstimate(
            flops=2 * slab * slab * half, bytes_accessed=4 * slab * half, transcendentals=0
        ),
        compiler_params=pltpu.CompilerParams(vmem_limit_bytes=VMEM_BYTES),
        name="place",
    )(side, order, values, *rest)


def down(x, by):
    return lax.ppermute(x, "pipe", [(i, i - by) for i in range(by, 4)])


def swap(x, axis):
    return lax.ppermute(x, axis, [(0, 1), (1, 0)])


def local(top_grad, slab_inputs, weights, master, moment1, moment2, grad_accum, layer_counts):
    sizes = [lax.axis_size(axis) for axis in DP_AXES]
    n_y, n_z, n_x, n_core = sizes
    section = lax.axis_index("pipe").astype(jnp.int32)
    core = lax.axis_index("core").astype(jnp.int32)
    rows, width = top_grad.shape
    slab = slab_inputs.shape[2]
    span = 4 * slab
    half = width // 2
    tokens = rows * n_y * n_z * n_x * n_core
    slab_own, weight = slab_inputs[0], weights[0]
    shard = master.shape[1:]

    state = jnp.concatenate([master, moment1, moment2, grad_accum] * 2)
    state = lax.all_gather(state, "z", axis=0, tiled=False)

    known = known_part(section[None], top_grad, weight, slab, span, 4)
    known_all = [known, down(known, 1), down(known, 2), down(known, 3)]

    late, _ = lax.optimization_barrier((top_grad, known))
    sent = lax.dynamic_slice(late, (0, (1 - core) * half), (rows, half))
    sent = jnp.concatenate([sent, slab_own], axis=1)
    other = swap(sent, "core")
    w_sent = lax.optimization_barrier((weight, other))[0]
    w_sent = w_sent[:, 2 * slab : span]
    w_one = lax.ppermute(w_sent, "pipe", [(2, 1), (1, 0)])
    w_two = lax.ppermute(w_sent, "pipe", [(2, 0)])

    here = jnp.arange(slab)
    source = here // (n_x * n_z) * (n_x * n_z) + here % n_z * n_x + here // n_z % n_x
    order = (here[None, :] == source[:, None]).astype(bf16)
    tail, slab_a, slab_b = tail_product(core[None], order, slab_own, top_grad, other, span)

    head, section_grad = relay(
        section[None], top_grad, known_all, [weight, w_one, w_two], slab, span
    )
    head_other = swap(head, "core")
    product = head_product(core[None], slab_a, slab_b, head, head_other, top_grad, other, tail)
    parts = lax.all_to_all(product, ("y", "x"), split_axis=0, concat_axis=0, tiled=True)
    row = lax.axis_index("z").astype(jnp.int32)
    parts = fold_chunks(
        row[None],
        grad_accum[0].reshape(1, half),
        parts.reshape(n_y * n_x, n_z, half),
        n_z,
        tokens,
    )
    parts = lax.all_to_all(parts, "z", split_axis=0, concat_axis=0, tiled=True)
    sums = lax.all_to_all(fold(parts), "z", split_axis=0, concat_axis=0, tiled=True)

    group = ("pipe", "y", "x", "core")
    count = lax.dynamic_slice(layer_counts, (section,), (1,))
    total_grad, squares = total_of(count, sums, tokens, lax.axis_size(group))
    squares, state = lax.optimization_barrier((squares, state))
    squares = lax.all_to_all(squares, group, split_axis=0, concat_axis=0, tiled=True)

    state = state.transpose(1, 0, 2, 3).reshape(8, n_z, half)
    fresh, factor = fresh_weights(squares, total_grad, state[:3])
    fresh = lax.all_gather(fresh, "y", axis=0, tiled=False)
    fresh = jnp.broadcast_to(fresh[None], (n_x, n_y, n_z, half))
    fresh = lax.all_to_all(fresh, "x", split_axis=0, concat_axis=0, tiled=True)
    fresh = fresh.reshape(slab, half)
    source = here % n_x * (n_y * n_z) + here // n_x
    order = (here[None, :] == source[:, None]).astype(bf16)
    fresh_other = swap(fresh, "core")
    new_weights = place(core[None], order, fresh, 2)
    new_weights = place(1 - core[None], order, fresh_other, 2, new_weights)

    own = lax.dynamic_slice(total_grad, (row, 0), (1, half)).reshape(shard)
    adam_step, new_master = adam(own, master[0], moment1[0], moment2[0], factor[0, 0])
    return (new_weights[None], adam_step[None], new_master[None], section_grad[None])


def solution(mesh):
    devices = mesh.devices
    split = Mesh(devices.reshape((devices.shape[0],) + DP_SIZES), ("pipe",) + DP_AXES)
    return jax.shard_map(
        local,
        mesh=split,
        in_specs=(
            P(DP_AXES, None),
            P("pipe", DP_AXES, None),
            P("pipe", None, None),
            P("pipe", DP_AXES, None),
            P("pipe", DP_AXES, None),
            P("pipe", DP_AXES, None),
            P("pipe", DP_AXES, None),
            P(),
        ),
        out_specs=(
            P("pipe", None, None),
            P("pipe", DP_AXES, None),
            P("pipe", DP_AXES, None),
            P("pipe", DP_AXES, None),
        ),
        check_vma=False,
    )
```

```python
import functools
import jax
import jax.numpy as jnp
from jax import lax
from jax.experimental import pallas as pl
from jax.experimental.pallas import tpu as pltpu
from jax.sharding import Mesh, PartitionSpec as P

beta_one = 0.9
beta_two = 0.95
bias_one = 1.0 - 0.9**20
bias_two = 1.0 - 0.95**20
epsilon = 1e-08
decay_rate = 0.1
learn_rate = 0.0003
clip_norm = 1.0

bf16 = jnp.bfloat16
f32 = jnp.float32
VMEM_BYTES = 16 * 2**20
DP_AXES = ("y", "z", "x", "core")
DP_SIZES = (2, 16, 4, 2)


def dot(a, b, dims):
    return lax.dot_general(a, b, (dims, ((), ())), preferred_element_type=f32)


def vmem_spec():
    return pl.BlockSpec(memory_space=pltpu.VMEM)


def known_kernel(section_ref, top_ref, weight_ref, out_ref, *, slab, span):
    step = pl.program_id(0)

    @pl.when(step == 0)
    def _():
        column = lax.broadcasted_iota(jnp.int32, top_ref.shape, 1)
        later = (column >= (section_ref[0] + 1) * slab) & (column < span)
        known = jnp.where(later, 0.0, top_ref[...].astype(f32)).astype(bf16)
        out_ref[...] = dot(known, weight_ref[...], ((1,), (1,)))

    @pl.when(step != 0)
    def _():
        out_ref[...] += dot(top_ref[...], weight_ref[...], ((1,), (1,)))


def known_part(section, top_grad, weight, slab, span, steps):
    rows, width = top_grad.shape
    block = width // steps
    return pl.pallas_call(
        functools.partial(known_kernel, slab=slab, span=span),
        grid_spec=pltpu.PrefetchScalarGridSpec(
            num_scalar_prefetch=1,
            grid=(steps,),
            in_specs=[
                pl.BlockSpec((rows, block), lambda i, s: (0, i)),
                pl.BlockSpec((slab, block), lambda i, s: (0, i)),
            ],
            out_specs=pl.BlockSpec((rows, slab), lambda i, s: (0, 0)),
        ),
        out_shape=jax.ShapeDtypeStruct((rows, slab), f32),
        compiler_params=pltpu.CompilerParams(vmem_limit_bytes=56 * 2**20),
        name="known_part",
    )(section, top_grad, weight)


def relay_kernel(section_ref, top_ref, own_ref, one_ref, two_ref, three_ref, w_own_ref, w_one_ref, w_two_ref, head_ref, grad_ref, *, slab):
    section = section_ref[0]
    known = (own_ref, one_ref, two_ref, three_ref)
    for u in range(3, -1, -1):
        @pl.when(section <= u)
        def _(u=u):
            offset = u - section
            total = known[3][...]
            for k in (2, 1, 0):
                total = jnp.where(offset == k, known[k][...], total)
            for v in range(u + 1, 4):
                block = slice(v * slab, (v + 1) * slab)
                weight = w_own_ref[:, block].astype(f32)
                if v >= 2:
                    narrow = slice((v - 2) * slab, (v - 1) * slab)
                    weight = jnp.where(offset == 1, w_one_ref[:, narrow].astype(f32), weight)
                if v == 3:
                    weight = jnp.where(offset == 2, w_two_ref[...].astype(f32), weight)
                total = total + dot(head_ref[:, block], weight.astype(bf16), ((1,), (1,)))
            branch = total.astype(bf16)
            here = slice(u * slab, (u + 1) * slab)
            top = top_ref[:, here]
            placed = (top.astype(f32) + branch.astype(f32)).astype(bf16)
            head_ref[:, here] = jnp.where(offset == 0, top.astype(f32), placed.astype(f32)).astype(bf16)
            grad_ref[...] = branch

        @pl.when(section > u)
        def _(u=u):
            here = slice(u * slab, (u + 1) * slab)
            head_ref[:, here] = top_ref[:, here]


def relay(section, top_grad, known, weights, slab, span):
    rows = top_grad.shape[0]
    first = pl.BlockSpec((rows, span), lambda i: (0, 0))
    return pl.pallas_call(
        functools.partial(relay_kernel, slab=slab),
        grid=(1,),
        in_specs=[pl.BlockSpec(memory_space=pltpu.SMEM), first]
        + [pl.BlockSpec((rows, slab), lambda i: (0, 0))] * 4
        + [pl.BlockSpec((slab, span), lambda i: (0, 0))]
        + [pl.BlockSpec((slab, span // 2), lambda i: (0, 0)), pl.BlockSpec((slab, slab), lambda i: (0, 0))],
        out_specs=[first, pl.BlockSpec((rows, slab), lambda i: (0, 0))],
        out_shape=[
            jax.ShapeDtypeStruct((rows, span), bf16),
            jax.ShapeDtypeStruct((rows, slab), bf16),
        ],
        compiler_params=pltpu.CompilerParams(vmem_limit_bytes=VMEM_BYTES),
        name="relay",
    )(section, top_grad, *known, *weights)


def turn_kernel(order_ref, a_in_ref, b_in_ref, a_ref, b_ref):
    a_ref[...] = dot(order_ref[...], a_in_ref[...], ((1,), (1,))).astype(bf16)
    b_ref[...] = dot(order_ref[...], b_in_ref[...], ((1,), (1,))).astype(bf16)


def tail_kernel(core_ref, order_ref, slab_a_ref, slab_b_ref, top_ref, other_ref, out_ref, a_ref, b_ref):
    @pl.when(pl.program_id(0) == 0)
    def _():
        turn_kernel(order_ref, slab_a_ref, slab_b_ref, a_ref, b_ref)

    out_ref[...] = (
        dot(a_ref[...], top_ref[...], ((1,), (0,))) + dot(b_ref[...], other_ref[...], ((1,), (0,)))
    ).astype(bf16)


def tail_product(core, order, slab_a, top_grad, other, span):
    rows, width = top_grad.shape
    slab = slab_a.shape[1]
    half = width // 2
    blocks = half // span
    whole = pl.BlockSpec((rows, slab), lambda i, c: (0, 0))
    turned = pl.BlockSpec((slab, rows), lambda i, c: (0, 0))
    return pl.pallas_call(
        tail_kernel,
        grid_spec=pltpu.PrefetchScalarGridSpec(
            num_scalar_prefetch=1,
            grid=(blocks - 1,),
            in_specs=[
                turned,
                whole,
                pl.BlockSpec((rows, slab), lambda i, c: (0, half // slab)),
                pl.BlockSpec((rows, span), lambda i, c: (0, c[0] * blocks + i + 1)),
                pl.BlockSpec((rows, span), lambda i, c: (0, i + 1)),
            ],
            out_specs=[pl.BlockSpec((slab, span), lambda i, c: (0, i + 1)), turned, turned],
        ),
        out_shape=[
            jax.ShapeDtypeStruct((slab, half), bf16),
            jax.ShapeDtypeStruct((slab, rows), bf16),
            jax.ShapeDtypeStruct((slab, rows), bf16),
        ],
        compiler_params=pltpu.CompilerParams(vmem_limit_bytes=VMEM_BYTES),
        name="tail_product",
    )(core, order, slab_a, other, top_grad, other)


def head_kernel(core_ref, a_ref, b_ref, head_a_ref, head_b_ref, top_ref, other_ref, tail_ref, out_ref):
    @pl.when(core_ref[0] == 0)
    def _():
        out_ref[...] = (
            dot(a_ref[...], head_a_ref[...], ((1,), (0,))) + dot(b_ref[...], head_b_ref[...], ((1,), (0,)))
        ).astype(bf16)

    @pl.when(core_ref[0] != 0)
    def _():
        out_ref[...] = (
            dot(a_ref[...], top_ref[...], ((1,), (0,))) + dot(b_ref[...], other_ref[...], ((1,), (0,)))
        ).astype(bf16)


def head_product(core, a, b, head_a, head_b, top_grad, other, tail):
    rows, span = head_a.shape
    slab = a.shape[0]
    blocks = top_grad.shape[1] // 2 // span
    turned = pl.BlockSpec((slab, rows), lambda i, c: (0, 0))
    first = pl.BlockSpec((rows, span), lambda i, c: (0, 0))
    return pl.pallas_call(
        head_kernel,
        grid_spec=pltpu.PrefetchScalarGridSpec(
            num_scalar_prefetch=1,
            grid=(1,),
            in_specs=[turned, turned, first, first, pl.BlockSpec((rows, span), lambda i, c: (0, c[0] * blocks)), first]
            + [pl.BlockSpec(memory_space=pl.ANY)],
            out_specs=pl.BlockSpec((slab, span), lambda i, c: (0, 0)),
        ),
        out_shape=jax.ShapeDtypeStruct(tail.shape, bf16),
        input_output_aliases={7: 0},
        compiler_params=pltpu.CompilerParams(vmem_limit_bytes=VMEM_BYTES),
        name="head_product",
    )(core, a, b, head_a, head_b, top_grad, other, tail)


def fold_kernel(parts_ref, out_ref, *, count):
    total = parts_ref[0].astype(f32)
    for i in range(1, count):
        total = total + parts_ref[i].astype(f32)
    for i in range(count):
        out_ref[i] = total.astype(bf16)


def fold(parts):
    return pl.pallas_call(
        functools.partial(fold_kernel, count=parts.shape[0]),
        in_specs=[vmem_spec()],
        out_specs=vmem_spec(),
        out_shape=jax.ShapeDtypeStruct(parts.shape, bf16),
        compiler_params=pltpu.CompilerParams(vmem_limit_bytes=VMEM_BYTES),
        name="fold",
    )(parts)


def fold_chunks_kernel(row_ref, accum_ref, parts_ref, out_ref, *, tokens):
    count, rows, _ = parts_ref.shape
    chunks, _, width = out_ref.shape
    own = lax.broadcasted_iota(jnp.int32, (rows, width), 0) == row_ref[0]
    for j in range(chunks):
        cols = slice(j * width, (j + 1) * width)
        total = jnp.where(own, accum_ref[:, cols] * tokens, 0.0)
        for i in range(count):
            total = total + parts_ref[i, :, cols].astype(f32)
        out_ref[j] = total.astype(bf16)


def fold_chunks(row, accum, parts, chunks, tokens):
    _, rows, width = parts.shape
    return pl.pallas_call(
        functools.partial(fold_chunks_kernel, tokens=float(tokens)),
        in_specs=[pl.BlockSpec(memory_space=pltpu.SMEM)] + [vmem_spec()] * 2,
        out_specs=vmem_spec(),
        out_shape=jax.ShapeDtypeStruct((chunks, rows, width // chunks), bf16),
        compiler_params=pltpu.CompilerParams(vmem_limit_bytes=VMEM_BYTES),
        name="fold_chunks",
    )(row, accum, parts)


def total_kernel(count_ref, sums_ref, total_ref, square_ref, *, chunks, tokens):
    rows, width = sums_ref.shape[1:]
    square = jnp.zeros((rows, width), f32)
    for j in range(chunks):
        cols = slice(j * width, (j + 1) * width)
        total = sums_ref[j].astype(f32) * (1.0 / tokens)
        total_ref[:, cols] = total
        square = square + total * total
    square_ref[...] = jnp.full(square_ref.shape, jnp.sum(square) * count_ref[0].astype(f32), f32)


def total_of(count, sums, tokens, peers):
    chunks, rows, width = sums.shape
    return pl.pallas_call(
        functools.partial(total_kernel, chunks=sums.shape[0], tokens=tokens),
        in_specs=[pl.BlockSpec(memory_space=pltpu.SMEM), vmem_spec()],
        out_specs=[vmem_spec()] * 2,
        out_shape=[
            jax.ShapeDtypeStruct((rows, chunks * width), f32),
            jax.ShapeDtypeStruct((peers, 8, 128), f32),
        ],
        compiler_params=pltpu.CompilerParams(vmem_limit_bytes=VMEM_BYTES),
        name="total_of",
    )(count, sums)


def adam(total_grad, master, moment1, moment2, clip_factor):
    clipped = clip_factor * total_grad
    moment_one = beta_one * moment1 + (1.0 - beta_one) * clipped
    moment_two = beta_two * moment2 + (1.0 - beta_two) * clipped * clipped
    step = moment_one / bias_one / (jnp.sqrt(moment_two / bias_two) + epsilon) + decay_rate * master
    return step, master - learn_rate * step


def fresh_kernel(squares_ref, total_ref, state_ref, out_ref, factor_ref):
    square_norm = jnp.sum(squares_ref[...], axis=0)[:1]
    clip_factor = jnp.minimum(1.0, clip_norm / jnp.sqrt(square_norm))
    factor_ref[...] = jnp.broadcast_to(clip_factor, factor_ref.shape)
    lanes = factor_ref.shape[1]
    for j in range(total_ref.shape[1] // lanes):
        cols = slice(j * lanes, (j + 1) * lanes)
        fresh = adam(
            total_ref[:, cols], state_ref[0, :, cols], state_ref[1, :, cols], state_ref[2, :, cols], clip_factor
        )[1].astype(bf16)
        for copy in range(out_ref.shape[0]):
            out_ref[copy, :, cols] = fresh


def fresh_weights(squares, total_grad, state, copies):
    return pl.pallas_call(
        fresh_kernel,
        in_specs=[vmem_spec()] * 3,
        out_specs=[vmem_spec()] * 2,
        out_shape=[
            jax.ShapeDtypeStruct((copies,) + total_grad.shape, bf16),
            jax.ShapeDtypeStruct((8, 128), f32),
        ],
        compiler_params=pltpu.CompilerParams(vmem_limit_bytes=VMEM_BYTES),
        name="fresh_weights",
    )(squares, total_grad, state)


def place_kernel(side_ref, order_ref, half_ref, *refs):
    out_ref = refs[-1]
    out_ref[...] = dot(order_ref[...], half_ref[...], ((1,), (0,))).astype(bf16)


def place(side, order, values, steps, into=None):
    slab, half = values.shape
    block = half // steps
    rest = [] if into is None else [into]
    return pl.pallas_call(
        place_kernel,
        grid_spec=pltpu.PrefetchScalarGridSpec(
            num_scalar_prefetch=1,
            grid=(steps,),
            in_specs=[
                pl.BlockSpec((slab, slab), lambda j, c: (0, 0)),
                pl.BlockSpec((slab, block), lambda j, c: (0, j)),
            ]
            + [pl.BlockSpec(memory_space=pl.ANY)] * len(rest),
            out_specs=pl.BlockSpec((slab, block), lambda j, c: (0, c[0] * steps + j)),
        ),
        out_shape=jax.ShapeDtypeStruct((slab, 2 * half), bf16),
        input_output_aliases={3: 0} if rest else {},
        cost_estimate=pl.CostEstimate(
            flops=2 * slab * slab * half, bytes_accessed=4 * slab * half, transcendentals=0
        ),
        compiler_params=pltpu.CompilerParams(vmem_limit_bytes=VMEM_BYTES),
        name="place",
    )(side, order, values, *rest)


def down(x, by):
    return lax.ppermute(x, "pipe", [(i, i - by) for i in range(by, 4)])


def swap(x, axis):
    return lax.ppermute(x, axis, [(0, 1), (1, 0)])


def local(top_grad, slab_inputs, weights, master, moment1, moment2, grad_accum, layer_counts):
    sizes = [lax.axis_size(axis) for axis in DP_AXES]
    n_y, n_z, n_x, n_core = sizes
    section = lax.axis_index("pipe").astype(jnp.int32)
    core = lax.axis_index("core").astype(jnp.int32)
    rows, width = top_grad.shape
    slab = slab_inputs.shape[2]
    span = 4 * slab
    half = width // 2
    tokens = rows * n_y * n_z * n_x * n_core
    slab_own, weight = slab_inputs[0], weights[0]
    shard = master.shape[1:]

    state = jnp.concatenate([master, moment1, moment2, grad_accum] * 2)
    state = lax.all_gather(state, "z", axis=0, tiled=False)

    w_one = lax.ppermute(weight[:, 2 * slab : span], "pipe", [(2, 1), (1, 0)])
    w_two = lax.ppermute(weight[:, 3 * slab : span], "pipe", [(2, 0)])
    known = known_part(section[None], top_grad, weight, slab, span, 4)
    known_all = [known, down(known, 1), down(known, 2), down(known, 3)]
    w_head = lax.optimization_barrier((weight, known))[0][:, :span]

    late, known_all, w_head, w_one, w_two = lax.optimization_barrier(
        (top_grad, known_all, w_head, w_one, w_two)
    )
    sent = lax.dynamic_slice(late, (0, (1 - core) * half), (rows, half))
    other = swap(jnp.concatenate([sent, slab_own], axis=1), "core")

    here = jnp.arange(slab)
    source = here // (n_x * n_z) * (n_x * n_z) + here % n_z * n_x + here // n_z % n_x
    order = (here[None, :] == source[:, None]).astype(bf16)
    tail, slab_a, slab_b = tail_product(core[None], order, slab_own, top_grad, other, span)

    head, section_grad = relay(
        section[None], top_grad, known_all, [w_head, w_one, w_two], slab, span
    )
    head_other = swap(head, "core")
    product = head_product(core[None], slab_a, slab_b, head, head_other, top_grad, other, tail)
    parts = lax.all_to_all(product, ("y", "x"), split_axis=0, concat_axis=0, tiled=True)
    row = lax.axis_index("z").astype(jnp.int32)
    parts = fold_chunks(
        row[None],
        grad_accum[0].reshape(1, half),
        parts.reshape(n_y * n_x, n_z, half),
        n_z,
        tokens,
    )
    parts = lax.all_to_all(parts, "z", split_axis=0, concat_axis=0, tiled=True)
    sums = lax.all_to_all(fold(parts), "z", split_axis=0, concat_axis=0, tiled=True)

    group = ("pipe", "y", "x", "core")
    count = lax.dynamic_slice(layer_counts, (section,), (1,))
    total_grad, squares = total_of(count, sums, tokens, lax.axis_size(group))
    squares, state = lax.optimization_barrier((squares, state))
    squares = lax.all_to_all(squares, group, split_axis=0, concat_axis=0, tiled=True)

    state = state.transpose(1, 0, 2, 3).reshape(8, n_z, half)
    fresh, factor = fresh_weights(squares, total_grad, state[:3], n_y * n_x)
    fresh = lax.all_to_all(fresh, ("y", "x"), split_axis=0, concat_axis=0, tiled=True)
    fresh = fresh.reshape(slab, half)
    source = here // (n_x * n_z) * (n_x * n_z) + here % n_x * n_z + here // n_x % n_z
    order = (here[None, :] == source[:, None]).astype(bf16)
    fresh_other = swap(fresh, "core")
    new_weights = place(core[None], order, fresh, 2)
    new_weights = place(1 - core[None], order, fresh_other, 2, new_weights)

    own = lax.dynamic_slice(total_grad, (row, 0), (1, half)).reshape(shard)
    adam_step, new_master = adam(own, master[0], moment1[0], moment2[0], factor[0, 0])
    return (new_weights[None], adam_step[None], new_master[None], section_grad[None])


def solution(mesh):
    devices = mesh.devices
    split = Mesh(devices.reshape((devices.shape[0],) + DP_SIZES), ("pipe",) + DP_AXES)
    return jax.shard_map(
        local,
        mesh=split,
        in_specs=(
            P(DP_AXES, None),
            P("pipe", DP_AXES, None),
            P("pipe", None, None),
            P("pipe", DP_AXES, None),
            P("pipe", DP_AXES, None),
            P("pipe", DP_AXES, None),
            P("pipe", DP_AXES, None),
            P(),
        ),
        out_specs=(
            P("pipe", None, None),
            P("pipe", DP_AXES, None),
            P("pipe", DP_AXES, None),
            P("pipe", DP_AXES, None),
        ),
        check_vma=False,
    )
```

```python
import functools
import jax
import jax.numpy as jnp
from jax import lax
from jax.experimental import pallas as pl
from jax.experimental.pallas import tpu as pltpu
from jax.sharding import Mesh, PartitionSpec as P

beta_one = 0.9
beta_two = 0.95
bias_one = 1.0 - 0.9**20
bias_two = 1.0 - 0.95**20
epsilon = 1e-08
decay_rate = 0.1
learn_rate = 0.0003
clip_norm = 1.0

bf16 = jnp.bfloat16
f32 = jnp.float32
VMEM_BYTES = 16 * 2**20
DP_AXES = ("y", "z", "x", "core")
DP_SIZES = (2, 16, 4, 2)


def dot(a, b, dims):
    return lax.dot_general(a, b, (dims, ((), ())), preferred_element_type=f32)


def vmem_spec():
    return pl.BlockSpec(memory_space=pltpu.VMEM)


def known_kernel(place_ref, top_ref, weight_ref, slab_ref, out_ref, one_ref, two_ref, three_ref, sent_ref, tops_ref, weights_ref, sems, *, slab, span, steps):
    rows, width = tops_ref.shape
    block, half = width // steps, width // 2
    section, core = place_ref[0], place_ref[1]

    def copies(step):
        cols = pl.ds(step * block, block)
        return (
            pltpu.make_async_copy(top_ref.at[:, cols], tops_ref.at[:, cols], sems.at[0, step]),
            pltpu.make_async_copy(weight_ref.at[:, cols], weights_ref.at[:, cols], sems.at[1, step]),
        )

    for step in range(steps):
        for copy in copies(step):
            copy.start()
    sent_ref[:, half:] = slab_ref[...]
    for step in range(steps):
        for copy in copies(step):
            copy.wait()
        start, end = step * block, (step + 1) * block
        if step == 0:
            column = lax.broadcasted_iota(jnp.int32, (rows, span), 1)
            later = column >= (section + 1) * slab
            known = jnp.where(later, 0.0, tops_ref[:, :span].astype(f32)).astype(bf16)
            total = dot(known, weights_ref[:, :span], ((1,), (1,)))
            one_ref[:, : 2 * slab] = weights_ref[:, 2 * slab : span]
            two_ref[:, :slab] = weights_ref[:, 3 * slab : span]
            start = span
        if start < end:
            total = total + dot(tops_ref[:, start:end], weights_ref[:, start:end], ((1,), (1,)))
    high = total.astype(bf16)
    low = (total - high.astype(f32)).astype(bf16)
    out_ref[...] = total
    for ref in (one_ref, two_ref, three_ref):
        end = ref.shape[1]
        ref[:, end - 2 * slab : end - slab] = high
        ref[:, end - slab :] = low

    @pl.when(core == 0)
    def _():
        sent_ref[:, :half] = tops_ref[:, half:]

    @pl.when(core != 0)
    def _():
        sent_ref[:, :half] = tops_ref[:, :half]


def known_part(place, top_grad, weight, slab_own, span, steps):
    rows, width = top_grad.shape
    slab = slab_own.shape[1]
    widths = [slab, 4 * slab, 3 * slab, 2 * slab, width // 2 + slab]
    types = [f32, bf16, bf16, bf16, bf16]
    return pl.pallas_call(
        functools.partial(known_kernel, slab=slab, span=span, steps=steps),
        in_specs=[
            pl.BlockSpec(memory_space=pltpu.SMEM),
            pl.BlockSpec(memory_space=pltpu.HBM),
            pl.BlockSpec(memory_space=pltpu.HBM),
            vmem_spec(),
        ],
        out_specs=[vmem_spec()] * 5,
        out_shape=[jax.ShapeDtypeStruct((rows, w), t) for w, t in zip(widths, types)],
        scratch_shapes=[
            pltpu.VMEM((rows, width), bf16),
            pltpu.VMEM((slab, width), bf16),
            pltpu.SemaphoreType.DMA((2, steps)),
        ],
        compiler_params=pltpu.CompilerParams(vmem_limit_bytes=56 * 2**20),
        name="known_part",
    )(place, top_grad, weight, slab_own)


def relay_kernel(section_ref, top_ref, own_ref, one_ref, two_ref, three_ref, w_own_ref, head_ref, grad_ref, *, slab):
    section = section_ref[0]

    def pair(ref):
        end = ref.shape[1]
        return ref[:, end - 2 * slab : end - slab].astype(f32) + ref[:, end - slab :].astype(f32)

    for u in range(3, -1, -1):
        @pl.when(section <= u)
        def _(u=u):
            offset = u - section
            total = pair(three_ref)
            total = jnp.where(offset == 2, pair(two_ref), total)
            total = jnp.where(offset == 1, pair(one_ref), total)
            total = jnp.where(offset == 0, own_ref[...], total)
            for v in range(u + 1, 4):
                block = slice(v * slab, (v + 1) * slab)
                weight = w_own_ref[:, block].astype(f32)
                if v >= 2:
                    narrow = slice((v - 2) * slab, (v - 1) * slab)
                    weight = jnp.where(offset == 1, one_ref[:, narrow].astype(f32), weight)
                if v == 3:
                    weight = jnp.where(offset == 2, two_ref[:, :slab].astype(f32), weight)
                total = total + dot(head_ref[:, block], weight.astype(bf16), ((1,), (1,)))
            branch = total.astype(bf16)
            here = slice(u * slab, (u + 1) * slab)
            top = top_ref[:, here]
            placed = (top.astype(f32) + branch.astype(f32)).astype(bf16)
            head_ref[:, here] = jnp.where(offset == 0, top.astype(f32), placed.astype(f32)).astype(bf16)
            grad_ref[...] = branch

        @pl.when(section > u)
        def _(u=u):
            here = slice(u * slab, (u + 1) * slab)
            head_ref[:, here] = top_ref[:, here]


def relay(section, top_grad, known, weight, slab, span):
    rows = top_grad.shape[0]
    first = pl.BlockSpec((rows, span), lambda i: (0, 0))
    return pl.pallas_call(
        functools.partial(relay_kernel, slab=slab),
        grid=(1,),
        in_specs=[pl.BlockSpec(memory_space=pltpu.SMEM), first]
        + [pl.BlockSpec(k.shape, lambda i: (0, 0)) for k in known]
        + [pl.BlockSpec((slab, span), lambda i: (0, 0))],
        out_specs=[first, pl.BlockSpec((rows, slab), lambda i: (0, 0))],
        out_shape=[
            jax.ShapeDtypeStruct((rows, span), bf16),
            jax.ShapeDtypeStruct((rows, slab), bf16),
        ],
        compiler_params=pltpu.CompilerParams(vmem_limit_bytes=VMEM_BYTES),
        name="relay",
    )(section, top_grad, *known, weight)


def turn_kernel(order_ref, a_in_ref, b_in_ref, a_ref, b_ref):
    a_ref[...] = dot(order_ref[...], a_in_ref[...], ((1,), (1,))).astype(bf16)
    b_ref[...] = dot(order_ref[...], b_in_ref[...], ((1,), (1,))).astype(bf16)


def tail_kernel(core_ref, order_ref, slab_a_ref, slab_b_ref, top_ref, other_ref, out_ref, a_ref, b_ref):
    @pl.when(pl.program_id(0) == 0)
    def _():
        turn_kernel(order_ref, slab_a_ref, slab_b_ref, a_ref, b_ref)

    out_ref[...] = (
        dot(a_ref[...], top_ref[...], ((1,), (0,))) + dot(b_ref[...], other_ref[...], ((1,), (0,)))
    ).astype(bf16)


def tail_product(core, order, slab_a, top_grad, other, span):
    rows, width = top_grad.shape
    slab = slab_a.shape[1]
    half = width // 2
    blocks = half // span
    whole = pl.BlockSpec((rows, slab), lambda i, c: (0, 0))
    turned = pl.BlockSpec((slab, rows), lambda i, c: (0, 0))
    return pl.pallas_call(
        tail_kernel,
        grid_spec=pltpu.PrefetchScalarGridSpec(
            num_scalar_prefetch=1,
            grid=(blocks - 1,),
            in_specs=[
                turned,
                whole,
                pl.BlockSpec((rows, slab), lambda i, c: (0, half // slab)),
                pl.BlockSpec((rows, span), lambda i, c: (0, c[0] * blocks + i + 1)),
                pl.BlockSpec((rows, span), lambda i, c: (0, i + 1)),
            ],
            out_specs=[pl.BlockSpec((slab, span), lambda i, c: (0, i + 1)), turned, turned],
        ),
        out_shape=[
            jax.ShapeDtypeStruct((slab, half), bf16),
            jax.ShapeDtypeStruct((slab, rows), bf16),
            jax.ShapeDtypeStruct((slab, rows), bf16),
        ],
        compiler_params=pltpu.CompilerParams(vmem_limit_bytes=VMEM_BYTES),
        name="tail_product",
    )(core, order, slab_a, other, top_grad, other)


def head_kernel(core_ref, a_ref, b_ref, head_a_ref, head_b_ref, top_ref, other_ref, tail_ref, out_ref):
    @pl.when(core_ref[0] == 0)
    def _():
        out_ref[...] = (
            dot(a_ref[...], head_a_ref[...], ((1,), (0,))) + dot(b_ref[...], head_b_ref[...], ((1,), (0,)))
        ).astype(bf16)

    @pl.when(core_ref[0] != 0)
    def _():
        out_ref[...] = (
            dot(a_ref[...], top_ref[...], ((1,), (0,))) + dot(b_ref[...], other_ref[...], ((1,), (0,)))
        ).astype(bf16)


def head_product(core, a, b, head_a, head_b, top_grad, other, tail):
    rows, span = head_a.shape
    slab = a.shape[0]
    blocks = top_grad.shape[1] // 2 // span
    turned = pl.BlockSpec((slab, rows), lambda i, c: (0, 0))
    first = pl.BlockSpec((rows, span), lambda i, c: (0, 0))
    return pl.pallas_call(
        head_kernel,
        grid_spec=pltpu.PrefetchScalarGridSpec(
            num_scalar_prefetch=1,
            grid=(1,),
            in_specs=[turned, turned, first, first, pl.BlockSpec((rows, span), lambda i, c: (0, c[0] * blocks)), first]
            + [pl.BlockSpec(memory_space=pl.ANY)],
            out_specs=pl.BlockSpec((slab, span), lambda i, c: (0, 0)),
        ),
        out_shape=jax.ShapeDtypeStruct(tail.shape, bf16),
        input_output_aliases={7: 0},
        compiler_params=pltpu.CompilerParams(vmem_limit_bytes=VMEM_BYTES),
        name="head_product",
    )(core, a, b, head_a, head_b, top_grad, other, tail)


def fold_kernel(parts_ref, out_ref, *, count):
    total = parts_ref[0].astype(f32)
    for i in range(1, count):
        total = total + parts_ref[i].astype(f32)
    for i in range(count):
        out_ref[i] = total.astype(bf16)


def fold(parts):
    return pl.pallas_call(
        functools.partial(fold_kernel, count=parts.shape[0]),
        in_specs=[vmem_spec()],
        out_specs=vmem_spec(),
        out_shape=jax.ShapeDtypeStruct(parts.shape, bf16),
        compiler_params=pltpu.CompilerParams(vmem_limit_bytes=VMEM_BYTES),
        name="fold",
    )(parts)


def fold_chunks_kernel(row_ref, accum_ref, parts_ref, out_ref, *, tokens):
    count, rows, _ = parts_ref.shape
    chunks, _, width = out_ref.shape
    own = lax.broadcasted_iota(jnp.int32, (rows, width), 0) == row_ref[0]
    for j in range(chunks):
        cols = slice(j * width, (j + 1) * width)
        total = jnp.where(own, accum_ref[:, cols] * tokens, 0.0)
        for i in range(count):
            total = total + parts_ref[i, :, cols].astype(f32)
        out_ref[j] = total.astype(bf16)


def fold_chunks(row, accum, parts, chunks, tokens):
    _, rows, width = parts.shape
    return pl.pallas_call(
        functools.partial(fold_chunks_kernel, tokens=float(tokens)),
        in_specs=[pl.BlockSpec(memory_space=pltpu.SMEM)] + [vmem_spec()] * 2,
        out_specs=vmem_spec(),
        out_shape=jax.ShapeDtypeStruct((chunks, rows, width // chunks), bf16),
        compiler_params=pltpu.CompilerParams(vmem_limit_bytes=VMEM_BYTES),
        name="fold_chunks",
    )(row, accum, parts)


def total_kernel(count_ref, sums_ref, total_ref, square_ref, *, chunks, tokens):
    rows, width = sums_ref.shape[1:]
    square = jnp.zeros((rows, width), f32)
    for j in range(chunks):
        cols = slice(j * width, (j + 1) * width)
        total = sums_ref[j].astype(f32) * (1.0 / tokens)
        total_ref[:, cols] = total
        square = square + total * total
    square_ref[...] = jnp.full(square_ref.shape, jnp.sum(square) * count_ref[0].astype(f32), f32)


def total_of(count, sums, tokens, peers):
    chunks, rows, width = sums.shape
    return pl.pallas_call(
        functools.partial(total_kernel, chunks=sums.shape[0], tokens=tokens),
        in_specs=[pl.BlockSpec(memory_space=pltpu.SMEM), vmem_spec()],
        out_specs=[vmem_spec()] * 2,
        out_shape=[
            jax.ShapeDtypeStruct((rows, chunks * width), f32),
            jax.ShapeDtypeStruct((peers, 8, 128), f32),
        ],
        compiler_params=pltpu.CompilerParams(vmem_limit_bytes=VMEM_BYTES),
        name="total_of",
    )(count, sums)


def adam(total_grad, master, moment1, moment2, clip_factor):
    clipped = clip_factor * total_grad
    moment_one = beta_one * moment1 + (1.0 - beta_one) * clipped
    moment_two = beta_two * moment2 + (1.0 - beta_two) * clipped * clipped
    step = moment_one / bias_one / (jnp.sqrt(moment_two / bias_two) + epsilon) + decay_rate * master
    return step, master - learn_rate * step


def fresh_kernel(squares_ref, total_ref, state_ref, out_ref, factor_ref):
    square_norm = jnp.sum(squares_ref[...], axis=0)[:1]
    clip_factor = jnp.minimum(1.0, clip_norm / jnp.sqrt(square_norm))
    factor_ref[...] = jnp.broadcast_to(clip_factor, factor_ref.shape)
    lanes = factor_ref.shape[1]
    for j in range(total_ref.shape[1] // lanes):
        cols = slice(j * lanes, (j + 1) * lanes)
        fresh = adam(
            total_ref[:, cols], state_ref[0, :, cols], state_ref[1, :, cols], state_ref[2, :, cols], clip_factor
        )[1].astype(bf16)
        for copy in range(out_ref.shape[0]):
            out_ref[copy, :, cols] = fresh


def fresh_weights(squares, total_grad, state, copies):
    return pl.pallas_call(
        fresh_kernel,
        in_specs=[vmem_spec()] * 3,
        out_specs=[vmem_spec()] * 2,
        out_shape=[
            jax.ShapeDtypeStruct((copies,) + total_grad.shape, bf16),
            jax.ShapeDtypeStruct((8, 128), f32),
        ],
        compiler_params=pltpu.CompilerParams(vmem_limit_bytes=VMEM_BYTES),
        name="fresh_weights",
    )(squares, total_grad, state)


def place_kernel(side_ref, order_ref, half_ref, *refs):
    out_ref = refs[-1]
    out_ref[...] = dot(order_ref[...], half_ref[...], ((1,), (0,))).astype(bf16)


def place(side, order, values, steps, into=None):
    slab, half = values.shape
    block = half // steps
    rest = [] if into is None else [into]
    return pl.pallas_call(
        place_kernel,
        grid_spec=pltpu.PrefetchScalarGridSpec(
            num_scalar_prefetch=1,
            grid=(steps,),
            in_specs=[
                pl.BlockSpec((slab, slab), lambda j, c: (0, 0)),
                pl.BlockSpec((slab, block), lambda j, c: (0, j)),
            ]
            + [pl.BlockSpec(memory_space=pl.ANY)] * len(rest),
            out_specs=pl.BlockSpec((slab, block), lambda j, c: (0, c[0] * steps + j)),
        ),
        out_shape=jax.ShapeDtypeStruct((slab, 2 * half), bf16),
        input_output_aliases={3: 0} if rest else {},
        cost_estimate=pl.CostEstimate(
            flops=2 * slab * slab * half, bytes_accessed=4 * slab * half, transcendentals=0
        ),
        compiler_params=pltpu.CompilerParams(vmem_limit_bytes=VMEM_BYTES),
        name="place",
    )(side, order, values, *rest)


def down(x, by):
    return lax.ppermute(x, "pipe", [(i, i - by) for i in range(by, 4)])


def swap(x, axis):
    return lax.ppermute(x, axis, [(0, 1), (1, 0)])


def local(top_grad, slab_inputs, weights, master, moment1, moment2, grad_accum, layer_counts):
    sizes = [lax.axis_size(axis) for axis in DP_AXES]
    n_y, n_z, n_x, n_core = sizes
    section = lax.axis_index("pipe").astype(jnp.int32)
    core = lax.axis_index("core").astype(jnp.int32)
    rows, width = top_grad.shape
    slab = slab_inputs.shape[2]
    span = 4 * slab
    half = width // 2
    tokens = rows * n_y * n_z * n_x * n_core
    slab_own, weight = slab_inputs[0], weights[0]
    shard = master.shape[1:]

    state = jnp.concatenate([master, moment1, moment2, grad_accum] * 2)
    state = lax.all_gather(state, "z", axis=0, tiled=False)

    known, one, two, three, sent = known_part(
        jnp.stack([section, core]), top_grad, weight, slab_own, span, 8
    )
    known_all = [known, down(one, 1), down(two, 2), down(three, 3)]
    other = swap(sent, "core")
    w_head = lax.optimization_barrier((weight, known))[0][:, :span]

    here = jnp.arange(slab)
    source = here // (n_x * n_z) * (n_x * n_z) + here % n_z * n_x + here // n_z % n_x
    order = (here[None, :] == source[:, None]).astype(bf16)
    tail, slab_a, slab_b = tail_product(core[None], order, slab_own, top_grad, other, span)

    head, section_grad = relay(section[None], top_grad, known_all, w_head, slab, span)
    head_other = swap(head, "core")
    product = head_product(core[None], slab_a, slab_b, head, head_other, top_grad, other, tail)
    parts = lax.all_to_all(product, ("y", "x"), split_axis=0, concat_axis=0, tiled=True)
    row = lax.axis_index("z").astype(jnp.int32)
    parts = fold_chunks(
        row[None],
        grad_accum[0].reshape(1, half),
        parts.reshape(n_y * n_x, n_z, half),
        n_z,
        tokens,
    )
    parts = lax.all_to_all(parts, "z", split_axis=0, concat_axis=0, tiled=True)
    sums = lax.all_to_all(fold(parts), "z", split_axis=0, concat_axis=0, tiled=True)

    group = ("pipe", "y", "x", "core")
    count = lax.dynamic_slice(layer_counts, (section,), (1,))
    total_grad, squares = total_of(count, sums, tokens, lax.axis_size(group))
    squares = lax.all_to_all(squares, group, split_axis=0, concat_axis=0, tiled=True)

    state = state.transpose(1, 0, 2, 3).reshape(8, n_z, half)
    fresh, factor = fresh_weights(squares, total_grad, state[:3], n_y * n_x)
    fresh = lax.all_to_all(fresh, ("y", "x"), split_axis=0, concat_axis=0, tiled=True)
    own = lax.dynamic_slice(total_grad, (row, 0), (1, half)).reshape(shard)
    adam_step, new_master = adam(own, master[0], moment1[0], moment2[0], factor[0, 0])
    fresh, adam_step, new_master = lax.optimization_barrier((fresh, adam_step, new_master))
    fresh = fresh.reshape(slab, half)
    source = here // (n_x * n_z) * (n_x * n_z) + here % n_x * n_z + here // n_x % n_z
    order = (here[None, :] == source[:, None]).astype(bf16)
    fresh_other = swap(fresh, "core")
    new_weights = place(core[None], order, fresh, 2)
    new_weights = place(1 - core[None], order, fresh_other, 2, new_weights)

    return (new_weights[None], adam_step[None], new_master[None], section_grad[None])


def solution(mesh):
    devices = mesh.devices
    split = Mesh(devices.reshape((devices.shape[0],) + DP_SIZES), ("pipe",) + DP_AXES)
    return jax.shard_map(
        local,
        mesh=split,
        in_specs=(
            P(DP_AXES, None),
            P("pipe", DP_AXES, None),
            P("pipe", None, None),
            P("pipe", DP_AXES, None),
            P("pipe", DP_AXES, None),
            P("pipe", DP_AXES, None),
            P("pipe", DP_AXES, None),
            P(),
        ),
        out_specs=(
            P("pipe", None, None),
            P("pipe", DP_AXES, None),
            P("pipe", DP_AXES, None),
            P("pipe", DP_AXES, None),
        ),
        check_vma=False,
    )
```

```python
import functools
import jax
import jax.numpy as jnp
from jax import lax
from jax.experimental import pallas as pl
from jax.experimental.pallas import tpu as pltpu
from jax.sharding import Mesh, PartitionSpec as P

beta_one = 0.9
beta_two = 0.95
bias_one = 1.0 - 0.9**20
bias_two = 1.0 - 0.95**20
epsilon = 1e-08
decay_rate = 0.1
learn_rate = 0.0003
clip_norm = 1.0

bf16 = jnp.bfloat16
f32 = jnp.float32
VMEM_BYTES = 16 * 2**20
DP_AXES = ("y", "z", "x", "core")
DP_SIZES = (2, 16, 4, 2)


def dot(a, b, dims):
    return lax.dot_general(a, b, (dims, ((), ())), preferred_element_type=f32)


def vmem_spec():
    return pl.BlockSpec(memory_space=pltpu.VMEM)


def known_kernel(section_ref, core_ref, top_ref, weight_ref, slab_ref, out_ref, one_ref, two_ref, three_ref, sent_ref, tops_ref, weights_ref, sems, *, slab, span, steps):
    rows, width = tops_ref.shape
    block, half = width // steps, width // 2
    section, core = section_ref[0], core_ref[0]

    def copies(step):
        cols = pl.ds(step * block, block)
        return (
            pltpu.make_async_copy(top_ref.at[:, cols], tops_ref.at[:, cols], sems.at[0, step]),
            pltpu.make_async_copy(weight_ref.at[:, cols], weights_ref.at[:, cols], sems.at[1, step]),
        )

    for step in range(steps):
        for copy in copies(step):
            copy.start()
    sent_ref[:, half:] = slab_ref[...]
    for step in range(steps):
        for copy in copies(step):
            copy.wait()
        start, end = step * block, (step + 1) * block
        if step == 0:
            column = lax.broadcasted_iota(jnp.int32, (rows, span), 1)
            later = column >= (section + 1) * slab
            known = jnp.where(later, 0.0, tops_ref[:, :span].astype(f32)).astype(bf16)
            total = dot(known, weights_ref[:, :span], ((1,), (1,)))
            one_ref[:, : 2 * slab] = weights_ref[:, 2 * slab : span]
            two_ref[:, :slab] = weights_ref[:, 3 * slab : span]
            start = span
        if start < end:
            total = total + dot(tops_ref[:, start:end], weights_ref[:, start:end], ((1,), (1,)))
    high = total.astype(bf16)
    low = (total - high.astype(f32)).astype(bf16)
    out_ref[...] = total
    for ref in (one_ref, two_ref, three_ref):
        end = ref.shape[1]
        ref[:, end - 2 * slab : end - slab] = high
        ref[:, end - slab :] = low

    @pl.when(core == 0)
    def _():
        sent_ref[:, :half] = tops_ref[:, half:]

    @pl.when(core != 0)
    def _():
        sent_ref[:, :half] = tops_ref[:, :half]


def known_part(section, core, top_grad, weight, slab_own, span, steps):
    rows, width = top_grad.shape
    slab = slab_own.shape[1]
    widths = [slab, 4 * slab, 3 * slab, 2 * slab, width // 2 + slab]
    types = [f32, bf16, bf16, bf16, bf16]
    return pl.pallas_call(
        functools.partial(known_kernel, slab=slab, span=span, steps=steps),
        in_specs=[
            pl.BlockSpec(memory_space=pltpu.SMEM),
            pl.BlockSpec(memory_space=pltpu.SMEM),
            pl.BlockSpec(memory_space=pltpu.HBM),
            pl.BlockSpec(memory_space=pltpu.HBM),
            vmem_spec(),
        ],
        out_specs=[vmem_spec()] * 5,
        out_shape=[jax.ShapeDtypeStruct((rows, w), t) for w, t in zip(widths, types)],
        scratch_shapes=[
            pltpu.VMEM((rows, width), bf16),
            pltpu.VMEM((slab, width), bf16),
            pltpu.SemaphoreType.DMA((2, steps)),
        ],
        compiler_params=pltpu.CompilerParams(vmem_limit_bytes=56 * 2**20),
        name="known_part",
    )(section, core, top_grad, weight, slab_own)


def relay_kernel(section_ref, top_ref, own_ref, one_ref, two_ref, three_ref, w_own_ref, head_ref, grad_ref, *, slab):
    section = section_ref[0]

    def pair(ref):
        end = ref.shape[1]
        return ref[:, end - 2 * slab : end - slab].astype(f32) + ref[:, end - slab :].astype(f32)

    for u in range(3, -1, -1):
        @pl.when(section <= u)
        def _(u=u):
            offset = u - section
            total = pair(three_ref)
            total = jnp.where(offset == 2, pair(two_ref), total)
            total = jnp.where(offset == 1, pair(one_ref), total)
            total = jnp.where(offset == 0, own_ref[...], total)
            for v in range(u + 1, 4):
                block = slice(v * slab, (v + 1) * slab)
                weight = w_own_ref[:, block].astype(f32)
                if v >= 2:
                    narrow = slice((v - 2) * slab, (v - 1) * slab)
                    weight = jnp.where(offset == 1, one_ref[:, narrow].astype(f32), weight)
                if v == 3:
                    weight = jnp.where(offset == 2, two_ref[:, :slab].astype(f32), weight)
                total = total + dot(head_ref[:, block], weight.astype(bf16), ((1,), (1,)))
            branch = total.astype(bf16)
            here = slice(u * slab, (u + 1) * slab)
            top = top_ref[:, here]
            placed = (top.astype(f32) + branch.astype(f32)).astype(bf16)
            head_ref[:, here] = jnp.where(offset == 0, top.astype(f32), placed.astype(f32)).astype(bf16)
            grad_ref[...] = branch

        @pl.when(section > u)
        def _(u=u):
            here = slice(u * slab, (u + 1) * slab)
            head_ref[:, here] = top_ref[:, here]


def relay(section, top_grad, known, weight, slab, span):
    rows = top_grad.shape[0]
    first = pl.BlockSpec((rows, span), lambda i: (0, 0))
    return pl.pallas_call(
        functools.partial(relay_kernel, slab=slab),
        grid=(1,),
        in_specs=[pl.BlockSpec(memory_space=pltpu.SMEM), first]
        + [pl.BlockSpec(k.shape, lambda i: (0, 0)) for k in known]
        + [pl.BlockSpec((slab, span), lambda i: (0, 0))],
        out_specs=[first, pl.BlockSpec((rows, slab), lambda i: (0, 0))],
        out_shape=[
            jax.ShapeDtypeStruct((rows, span), bf16),
            jax.ShapeDtypeStruct((rows, slab), bf16),
        ],
        compiler_params=pltpu.CompilerParams(vmem_limit_bytes=VMEM_BYTES),
        name="relay",
    )(section, top_grad, *known, weight)


def turn_kernel(order_ref, a_in_ref, b_in_ref, a_ref, b_ref):
    a_ref[...] = dot(order_ref[...], a_in_ref[...], ((1,), (1,))).astype(bf16)
    b_ref[...] = dot(order_ref[...], b_in_ref[...], ((1,), (1,))).astype(bf16)


def tail_kernel(core_ref, order_ref, slab_a_ref, slab_b_ref, top_ref, other_ref, out_ref, a_ref, b_ref):
    @pl.when(pl.program_id(0) == 0)
    def _():
        turn_kernel(order_ref, slab_a_ref, slab_b_ref, a_ref, b_ref)

    out_ref[...] = (
        dot(a_ref[...], top_ref[...], ((1,), (0,))) + dot(b_ref[...], other_ref[...], ((1,), (0,)))
    ).astype(bf16)


def tail_product(core, order, slab_a, top_grad, other, span):
    rows, width = top_grad.shape
    slab = slab_a.shape[1]
    half = width // 2
    blocks = half // span
    whole = pl.BlockSpec((rows, slab), lambda i, c: (0, 0))
    turned = pl.BlockSpec((slab, rows), lambda i, c: (0, 0))
    return pl.pallas_call(
        tail_kernel,
        grid_spec=pltpu.PrefetchScalarGridSpec(
            num_scalar_prefetch=1,
            grid=(blocks - 1,),
            in_specs=[
                turned,
                whole,
                pl.BlockSpec((rows, slab), lambda i, c: (0, half // slab)),
                pl.BlockSpec((rows, span), lambda i, c: (0, c[0] * blocks + i + 1)),
                pl.BlockSpec((rows, span), lambda i, c: (0, i + 1)),
            ],
            out_specs=[pl.BlockSpec((slab, span), lambda i, c: (0, i + 1)), turned, turned],
        ),
        out_shape=[
            jax.ShapeDtypeStruct((slab, half), bf16),
            jax.ShapeDtypeStruct((slab, rows), bf16),
            jax.ShapeDtypeStruct((slab, rows), bf16),
        ],
        compiler_params=pltpu.CompilerParams(vmem_limit_bytes=VMEM_BYTES),
        name="tail_product",
    )(core, order, slab_a, other, top_grad, other)


def head_kernel(core_ref, a_ref, b_ref, head_a_ref, head_b_ref, top_ref, other_ref, tail_ref, out_ref):
    @pl.when(core_ref[0] == 0)
    def _():
        out_ref[...] = (
            dot(a_ref[...], head_a_ref[...], ((1,), (0,))) + dot(b_ref[...], head_b_ref[...], ((1,), (0,)))
        ).astype(bf16)

    @pl.when(core_ref[0] != 0)
    def _():
        out_ref[...] = (
            dot(a_ref[...], top_ref[...], ((1,), (0,))) + dot(b_ref[...], other_ref[...], ((1,), (0,)))
        ).astype(bf16)


def head_product(core, a, b, head_a, head_b, top_grad, other, tail):
    rows, span = head_a.shape
    slab = a.shape[0]
    blocks = top_grad.shape[1] // 2 // span
    turned = pl.BlockSpec((slab, rows), lambda i, c: (0, 0))
    first = pl.BlockSpec((rows, span), lambda i, c: (0, 0))
    return pl.pallas_call(
        head_kernel,
        grid_spec=pltpu.PrefetchScalarGridSpec(
            num_scalar_prefetch=1,
            grid=(1,),
            in_specs=[turned, turned, first, first, pl.BlockSpec((rows, span), lambda i, c: (0, c[0] * blocks)), first]
            + [pl.BlockSpec(memory_space=pl.ANY)],
            out_specs=pl.BlockSpec((slab, span), lambda i, c: (0, 0)),
        ),
        out_shape=jax.ShapeDtypeStruct(tail.shape, bf16),
        input_output_aliases={7: 0},
        compiler_params=pltpu.CompilerParams(vmem_limit_bytes=VMEM_BYTES),
        name="head_product",
    )(core, a, b, head_a, head_b, top_grad, other, tail)


def fold_kernel(parts_ref, out_ref, *, count):
    total = parts_ref[0].astype(f32)
    for i in range(1, count):
        total = total + parts_ref[i].astype(f32)
    for i in range(count):
        out_ref[i] = total.astype(bf16)


def fold(parts):
    return pl.pallas_call(
        functools.partial(fold_kernel, count=parts.shape[0]),
        in_specs=[vmem_spec()],
        out_specs=vmem_spec(),
        out_shape=jax.ShapeDtypeStruct(parts.shape, bf16),
        compiler_params=pltpu.CompilerParams(vmem_limit_bytes=VMEM_BYTES),
        name="fold",
    )(parts)


def fold_chunks_kernel(row_ref, accum_ref, parts_ref, out_ref, *, tokens):
    count, rows, _ = parts_ref.shape
    chunks, _, width = out_ref.shape
    own = lax.broadcasted_iota(jnp.int32, (rows, width), 0) == row_ref[0]
    for j in range(chunks):
        cols = slice(j * width, (j + 1) * width)
        total = jnp.where(own, accum_ref[:, cols] * tokens, 0.0)
        for i in range(count):
            total = total + parts_ref[i, :, cols].astype(f32)
        out_ref[j] = total.astype(bf16)


def fold_chunks(row, accum, parts, chunks, tokens):
    _, rows, width = parts.shape
    return pl.pallas_call(
        functools.partial(fold_chunks_kernel, tokens=float(tokens)),
        in_specs=[pl.BlockSpec(memory_space=pltpu.SMEM)] + [vmem_spec()] * 2,
        out_specs=vmem_spec(),
        out_shape=jax.ShapeDtypeStruct((chunks, rows, width // chunks), bf16),
        compiler_params=pltpu.CompilerParams(vmem_limit_bytes=VMEM_BYTES),
        name="fold_chunks",
    )(row, accum, parts)


def total_kernel(count_ref, sums_ref, total_ref, square_ref, *, chunks, tokens):
    rows, width = sums_ref.shape[1:]
    square = jnp.zeros((rows, width), f32)
    for j in range(chunks):
        cols = slice(j * width, (j + 1) * width)
        total = sums_ref[j].astype(f32) * (1.0 / tokens)
        total_ref[:, cols] = total
        square = square + total * total
    square_ref[...] = jnp.full(square_ref.shape, jnp.sum(square) * count_ref[0].astype(f32), f32)


def total_of(count, sums, tokens, peers):
    chunks, rows, width = sums.shape
    return pl.pallas_call(
        functools.partial(total_kernel, chunks=sums.shape[0], tokens=tokens),
        in_specs=[pl.BlockSpec(memory_space=pltpu.SMEM), vmem_spec()],
        out_specs=[vmem_spec()] * 2,
        out_shape=[
            jax.ShapeDtypeStruct((rows, chunks * width), f32),
            jax.ShapeDtypeStruct((peers, 1, 128), f32),
        ],
        compiler_params=pltpu.CompilerParams(vmem_limit_bytes=VMEM_BYTES),
        name="total_of",
    )(count, sums)


def adam(total_grad, master, moment1, moment2, clip_factor):
    clipped = clip_factor * total_grad
    moment_one = beta_one * moment1 + (1.0 - beta_one) * clipped
    moment_two = beta_two * moment2 + (1.0 - beta_two) * clipped * clipped
    step = moment_one / bias_one / (jnp.sqrt(moment_two / bias_two) + epsilon) + decay_rate * master
    return step, master - learn_rate * step


def fresh_kernel(squares_ref, total_ref, state_ref, out_ref, factor_ref):
    square_norm = jnp.sum(squares_ref[...], axis=0)
    clip_factor = jnp.minimum(1.0, clip_norm / jnp.sqrt(square_norm))
    factor_ref[...] = jnp.broadcast_to(clip_factor, factor_ref.shape)
    lanes = factor_ref.shape[1]
    for j in range(total_ref.shape[1] // lanes):
        cols = slice(j * lanes, (j + 1) * lanes)
        fresh = adam(
            total_ref[:, cols], state_ref[0, :, cols], state_ref[1, :, cols], state_ref[2, :, cols], clip_factor
        )[1].astype(bf16)
        for copy in range(out_ref.shape[0]):
            out_ref[copy, :, cols] = fresh


def fresh_weights(squares, total_grad, state, copies):
    return pl.pallas_call(
        fresh_kernel,
        in_specs=[vmem_spec()] * 3,
        out_specs=[vmem_spec()] * 2,
        out_shape=[
            jax.ShapeDtypeStruct((copies,) + total_grad.shape, bf16),
            jax.ShapeDtypeStruct((8, 128), f32),
        ],
        compiler_params=pltpu.CompilerParams(vmem_limit_bytes=VMEM_BYTES),
        name="fresh_weights",
    )(squares, total_grad, state)


def place_kernel(side_ref, order_ref, half_ref, *refs):
    out_ref = refs[-1]
    out_ref[...] = dot(order_ref[...], half_ref[...], ((1,), (0,))).astype(bf16)


def place(side, order, values, steps, into=None):
    slab, half = values.shape
    block = half // steps
    rest = [] if into is None else [into]
    return pl.pallas_call(
        place_kernel,
        grid_spec=pltpu.PrefetchScalarGridSpec(
            num_scalar_prefetch=1,
            grid=(steps,),
            in_specs=[
                pl.BlockSpec((slab, slab), lambda j, c: (0, 0)),
                pl.BlockSpec((slab, block), lambda j, c: (0, j)),
            ]
            + [pl.BlockSpec(memory_space=pl.ANY)] * len(rest),
            out_specs=pl.BlockSpec((slab, block), lambda j, c: (0, c[0] * steps + j)),
        ),
        out_shape=jax.ShapeDtypeStruct((slab, 2 * half), bf16),
        input_output_aliases={3: 0} if rest else {},
        cost_estimate=pl.CostEstimate(
            flops=2 * slab * slab * half, bytes_accessed=4 * slab * half, transcendentals=0
        ),
        compiler_params=pltpu.CompilerParams(vmem_limit_bytes=VMEM_BYTES),
        name="place",
    )(side, order, values, *rest)


def down(x, by):
    return lax.ppermute(x, "pipe", [(i, i - by) for i in range(by, 4)])


def swap(x, axis):
    return lax.ppermute(x, axis, [(0, 1), (1, 0)])


def local(top_grad, slab_inputs, weights, master, moment1, moment2, grad_accum, layer_counts):
    sizes = [lax.axis_size(axis) for axis in DP_AXES]
    n_y, n_z, n_x, n_core = sizes
    section = lax.axis_index("pipe").astype(jnp.int32)
    core = lax.axis_index("core").astype(jnp.int32)
    rows, width = top_grad.shape
    slab = slab_inputs.shape[2]
    span = 4 * slab
    half = width // 2
    tokens = rows * n_y * n_z * n_x * n_core
    slab_own, weight = slab_inputs[0], weights[0]
    shard = master.shape[1:]

    state = jnp.concatenate([master, moment1, moment2, grad_accum] * 2)
    state = lax.all_gather(state, "z", axis=0, tiled=False)

    known, one, two, three, sent = known_part(
        section[None], core[None], top_grad, weight, slab_own, span, 4
    )
    known_all = [known, down(one, 1), down(two, 2), down(three, 3)]
    other = swap(sent, "core")
    w_head = lax.optimization_barrier((weight, known))[0][:, :span]

    here = jnp.arange(slab)
    source = here // (n_x * n_z) * (n_x * n_z) + here % n_z * n_x + here // n_z % n_x
    order = (here[None, :] == source[:, None]).astype(bf16)
    tail, slab_a, slab_b = tail_product(core[None], order, slab_own, top_grad, other, span)

    head, section_grad = relay(section[None], top_grad, known_all, w_head, slab, span)
    head_other = swap(head, "core")
    product = head_product(core[None], slab_a, slab_b, head, head_other, top_grad, other, tail)
    parts = lax.all_to_all(product, ("y", "x"), split_axis=0, concat_axis=0, tiled=True)
    row = lax.axis_index("z").astype(jnp.int32)
    parts = fold_chunks(
        row[None],
        grad_accum[0].reshape(1, half),
        parts.reshape(n_y * n_x, n_z, half),
        n_z,
        tokens,
    )
    parts = lax.all_to_all(parts, "z", split_axis=0, concat_axis=0, tiled=True)
    sums = lax.all_to_all(fold(parts), "z", split_axis=0, concat_axis=0, tiled=True)

    group = ("pipe", "y", "x", "core")
    count = lax.dynamic_slice(layer_counts, (section,), (1,))
    total_grad, squares = total_of(count, sums, tokens, lax.axis_size(group))
    squares = lax.all_to_all(squares, group, split_axis=0, concat_axis=0, tiled=True)

    state = state.transpose(1, 0, 2, 3).reshape(8, n_z, half)
    fresh, factor = fresh_weights(squares, total_grad, state[:3], n_y * n_x)
    fresh = lax.all_to_all(fresh, ("y", "x"), split_axis=0, concat_axis=0, tiled=True)
    own = lax.dynamic_slice(total_grad, (row, 0), (1, half)).reshape(shard)
    adam_step, new_master = adam(own, master[0], moment1[0], moment2[0], factor[0, 0])
    fresh, adam_step, new_master = lax.optimization_barrier((fresh, adam_step, new_master))
    fresh = fresh.reshape(slab, half)
    source = here // (n_x * n_z) * (n_x * n_z) + here % n_x * n_z + here // n_x % n_z
    order = (here[None, :] == source[:, None]).astype(bf16)
    fresh_other = swap(fresh, "core")
    new_weights = place(core[None], order, fresh, 2)
    new_weights = place(1 - core[None], order, fresh_other, 2, new_weights)

    return (new_weights[None], adam_step[None], new_master[None], section_grad[None])


def solution(mesh):
    devices = mesh.devices
    split = Mesh(devices.reshape((devices.shape[0],) + DP_SIZES), ("pipe",) + DP_AXES)
    return jax.shard_map(
        local,
        mesh=split,
        in_specs=(
            P(DP_AXES, None),
            P("pipe", DP_AXES, None),
            P("pipe", None, None),
            P("pipe", DP_AXES, None),
            P("pipe", DP_AXES, None),
            P("pipe", DP_AXES, None),
            P("pipe", DP_AXES, None),
            P(),
        ),
        out_specs=(
            P("pipe", None, None),
            P("pipe", DP_AXES, None),
            P("pipe", DP_AXES, None),
            P("pipe", DP_AXES, None),
        ),
        check_vma=False,
    )
```

```python
import functools
import jax
import jax.numpy as jnp
from jax import lax
from jax.experimental import pallas as pl
from jax.experimental.pallas import tpu as pltpu
from jax.sharding import Mesh, PartitionSpec as P

beta_one = 0.9
beta_two = 0.95
bias_one = 1.0 - 0.9**20
bias_two = 1.0 - 0.95**20
epsilon = 1e-08
decay_rate = 0.1
learn_rate = 0.0003
clip_norm = 1.0

bf16 = jnp.bfloat16
f32 = jnp.float32
VMEM_BYTES = 16 * 2**20
DP_AXES = ("y", "z", "x", "core")
DP_SIZES = (2, 16, 4, 2)


def dot(a, b, dims):
    return lax.dot_general(a, b, (dims, ((), ())), preferred_element_type=f32)


def vmem_spec():
    return pl.BlockSpec(memory_space=pltpu.VMEM)


def known_kernel(section_ref, core_ref, top_ref, weight_ref, slab_ref, share_a, share_b, share_c, share_d, out_ref, one_ref, two_ref, three_ref, sent_ref, state_ref, tops_ref, weights_ref, sems, *, slab, span, steps):
    rows, width = tops_ref.shape
    block, half = width // steps, width // 2
    section, core = section_ref[0], core_ref[0]

    def copies(step):
        cols = pl.ds(step * block, block)
        return (
            pltpu.make_async_copy(top_ref.at[:, cols], tops_ref.at[:, cols], sems.at[0, step]),
            pltpu.make_async_copy(weight_ref.at[:, cols], weights_ref.at[:, cols], sems.at[1, step]),
        )

    for step in range(steps):
        for copy in copies(step):
            copy.start()
    sent_ref[:, half:] = slab_ref[...]
    for i, share in enumerate((share_a, share_b, share_c, share_d) * 2):
        state_ref[i] = share[...]
    for step in range(steps):
        for copy in copies(step):
            copy.wait()
        start, end = step * block, (step + 1) * block
        if step == 0:
            column = lax.broadcasted_iota(jnp.int32, (rows, span), 1)
            later = column >= (section + 1) * slab
            known = jnp.where(later, 0.0, tops_ref[:, :span].astype(f32)).astype(bf16)
            total = dot(known, weights_ref[:, :span], ((1,), (1,)))
            one_ref[:, : 2 * slab] = weights_ref[:, 2 * slab : span]
            two_ref[:, :slab] = weights_ref[:, 3 * slab : span]
            start = span
        if start < end:
            total = total + dot(tops_ref[:, start:end], weights_ref[:, start:end], ((1,), (1,)))
    high = total.astype(bf16)
    low = (total - high.astype(f32)).astype(bf16)
    out_ref[...] = total
    for ref in (one_ref, two_ref, three_ref):
        end = ref.shape[1]
        ref[:, end - 2 * slab : end - slab] = high
        ref[:, end - slab :] = low

    @pl.when(core == 0)
    def _():
        sent_ref[:, :half] = tops_ref[:, half:]

    @pl.when(core != 0)
    def _():
        sent_ref[:, :half] = tops_ref[:, :half]


def known_part(section, core, top_grad, weight, slab_own, shares, span, steps):
    rows, width = top_grad.shape
    slab = slab_own.shape[1]
    widths = [slab, 4 * slab, 3 * slab, 2 * slab, width // 2 + slab]
    types = [f32, bf16, bf16, bf16, bf16]
    return pl.pallas_call(
        functools.partial(known_kernel, slab=slab, span=span, steps=steps),
        in_specs=[
            pl.BlockSpec(memory_space=pltpu.SMEM),
            pl.BlockSpec(memory_space=pltpu.SMEM),
            pl.BlockSpec(memory_space=pltpu.HBM),
            pl.BlockSpec(memory_space=pltpu.HBM),
        ]
        + [vmem_spec()] * 5,
        out_specs=[vmem_spec()] * 6,
        out_shape=[jax.ShapeDtypeStruct((rows, w), t) for w, t in zip(widths, types)]
        + [jax.ShapeDtypeStruct((8,) + shares[0].shape, f32)],
        scratch_shapes=[
            pltpu.VMEM((rows, width), bf16),
            pltpu.VMEM((slab, width), bf16),
            pltpu.SemaphoreType.DMA((2, steps)),
        ],
        compiler_params=pltpu.CompilerParams(vmem_limit_bytes=56 * 2**20),
        name="known_part",
    )(section, core, top_grad, weight, slab_own, *shares)


def relay_kernel(section_ref, top_ref, own_ref, one_ref, two_ref, three_ref, w_own_ref, head_ref, grad_ref, *, slab):
    section = section_ref[0]

    def pair(ref):
        end = ref.shape[1]
        return ref[:, end - 2 * slab : end - slab].astype(f32) + ref[:, end - slab :].astype(f32)

    for u in range(3, -1, -1):
        @pl.when(section <= u)
        def _(u=u):
            offset = u - section
            total = pair(three_ref)
            total = jnp.where(offset == 2, pair(two_ref), total)
            total = jnp.where(offset == 1, pair(one_ref), total)
            total = jnp.where(offset == 0, own_ref[...], total)
            for v in range(u + 1, 4):
                block = slice(v * slab, (v + 1) * slab)
                weight = w_own_ref[:, block].astype(f32)
                if v >= 2:
                    narrow = slice((v - 2) * slab, (v - 1) * slab)
                    weight = jnp.where(offset == 1, one_ref[:, narrow].astype(f32), weight)
                if v == 3:
                    weight = jnp.where(offset == 2, two_ref[:, :slab].astype(f32), weight)
                total = total + dot(head_ref[:, block], weight.astype(bf16), ((1,), (1,)))
            branch = total.astype(bf16)
            here = slice(u * slab, (u + 1) * slab)
            top = top_ref[:, here]
            placed = (top.astype(f32) + branch.astype(f32)).astype(bf16)
            head_ref[:, here] = jnp.where(offset == 0, top.astype(f32), placed.astype(f32)).astype(bf16)
            grad_ref[...] = branch

        @pl.when(section > u)
        def _(u=u):
            here = slice(u * slab, (u + 1) * slab)
            head_ref[:, here] = top_ref[:, here]


def relay(section, top_grad, known, weight, slab, span):
    rows = top_grad.shape[0]
    first = pl.BlockSpec((rows, span), lambda i: (0, 0))
    return pl.pallas_call(
        functools.partial(relay_kernel, slab=slab),
        grid=(1,),
        in_specs=[pl.BlockSpec(memory_space=pltpu.SMEM), first]
        + [pl.BlockSpec(k.shape, lambda i: (0, 0)) for k in known]
        + [pl.BlockSpec((slab, span), lambda i: (0, 0))],
        out_specs=[first, pl.BlockSpec((rows, slab), lambda i: (0, 0))],
        out_shape=[
            jax.ShapeDtypeStruct((rows, span), bf16),
            jax.ShapeDtypeStruct((rows, slab), bf16),
        ],
        compiler_params=pltpu.CompilerParams(vmem_limit_bytes=VMEM_BYTES),
        name="relay",
    )(section, top_grad, *known, weight)


def turn_kernel(order_ref, a_in_ref, b_in_ref, a_ref, b_ref):
    a_ref[...] = dot(order_ref[...], a_in_ref[...], ((1,), (1,))).astype(bf16)
    b_ref[...] = dot(order_ref[...], b_in_ref[...], ((1,), (1,))).astype(bf16)


def tail_kernel(core_ref, order_ref, slab_a_ref, slab_b_ref, top_ref, other_ref, out_ref, a_ref, b_ref):
    @pl.when(pl.program_id(0) == 0)
    def _():
        turn_kernel(order_ref, slab_a_ref, slab_b_ref, a_ref, b_ref)

    out_ref[...] = (
        dot(a_ref[...], top_ref[...], ((1,), (0,))) + dot(b_ref[...], other_ref[...], ((1,), (0,)))
    ).astype(bf16)


def tail_product(core, order, slab_a, top_grad, other, span):
    rows, width = top_grad.shape
    slab = slab_a.shape[1]
    half = width // 2
    blocks = half // span
    whole = pl.BlockSpec((rows, slab), lambda i, c: (0, 0))
    turned = pl.BlockSpec((slab, rows), lambda i, c: (0, 0))
    return pl.pallas_call(
        tail_kernel,
        grid_spec=pltpu.PrefetchScalarGridSpec(
            num_scalar_prefetch=1,
            grid=(blocks - 1,),
            in_specs=[
                turned,
                whole,
                pl.BlockSpec((rows, slab), lambda i, c: (0, half // slab)),
                pl.BlockSpec((rows, span), lambda i, c: (0, c[0] * blocks + i + 1)),
                pl.BlockSpec((rows, span), lambda i, c: (0, i + 1)),
            ],
            out_specs=[pl.BlockSpec((slab, span), lambda i, c: (0, i + 1)), turned, turned],
        ),
        out_shape=[
            jax.ShapeDtypeStruct((slab, half), bf16),
            jax.ShapeDtypeStruct((slab, rows), bf16),
            jax.ShapeDtypeStruct((slab, rows), bf16),
        ],
        compiler_params=pltpu.CompilerParams(vmem_limit_bytes=VMEM_BYTES),
        name="tail_product",
    )(core, order, slab_a, other, top_grad, other)


def head_kernel(core_ref, a_ref, b_ref, head_a_ref, head_b_ref, top_ref, other_ref, tail_ref, out_ref):
    @pl.when(core_ref[0] == 0)
    def _():
        out_ref[...] = (
            dot(a_ref[...], head_a_ref[...], ((1,), (0,))) + dot(b_ref[...], head_b_ref[...], ((1,), (0,)))
        ).astype(bf16)

    @pl.when(core_ref[0] != 0)
    def _():
        out_ref[...] = (
            dot(a_ref[...], top_ref[...], ((1,), (0,))) + dot(b_ref[...], other_ref[...], ((1,), (0,)))
        ).astype(bf16)


def head_product(core, a, b, head_a, head_b, top_grad, other, tail):
    rows, span = head_a.shape
    slab = a.shape[0]
    blocks = top_grad.shape[1] // 2 // span
    turned = pl.BlockSpec((slab, rows), lambda i, c: (0, 0))
    first = pl.BlockSpec((rows, span), lambda i, c: (0, 0))
    return pl.pallas_call(
        head_kernel,
        grid_spec=pltpu.PrefetchScalarGridSpec(
            num_scalar_prefetch=1,
            grid=(1,),
            in_specs=[turned, turned, first, first, pl.BlockSpec((rows, span), lambda i, c: (0, c[0] * blocks)), first]
            + [pl.BlockSpec(memory_space=pl.ANY)],
            out_specs=pl.BlockSpec((slab, span), lambda i, c: (0, 0)),
        ),
        out_shape=jax.ShapeDtypeStruct(tail.shape, bf16),
        input_output_aliases={7: 0},
        compiler_params=pltpu.CompilerParams(vmem_limit_bytes=VMEM_BYTES),
        name="head_product",
    )(core, a, b, head_a, head_b, top_grad, other, tail)


def fold_kernel(parts_ref, out_ref, *, count):
    total = parts_ref[0].astype(f32)
    for i in range(1, count):
        total = total + parts_ref[i].astype(f32)
    for i in range(count):
        out_ref[i] = total.astype(bf16)


def fold(parts):
    return pl.pallas_call(
        functools.partial(fold_kernel, count=parts.shape[0]),
        in_specs=[vmem_spec()],
        out_specs=vmem_spec(),
        out_shape=jax.ShapeDtypeStruct(parts.shape, bf16),
        compiler_params=pltpu.CompilerParams(vmem_limit_bytes=VMEM_BYTES),
        name="fold",
    )(parts)


def fold_chunks_kernel(row_ref, accum_ref, parts_ref, out_ref, *, tokens):
    count, rows, _ = parts_ref.shape
    chunks, _, width = out_ref.shape
    own = lax.broadcasted_iota(jnp.int32, (rows, width), 0) == row_ref[0]
    for j in range(chunks):
        cols = slice(j * width, (j + 1) * width)
        total = jnp.where(own, accum_ref[:, cols] * tokens, 0.0)
        for i in range(count):
            total = total + parts_ref[i, :, cols].astype(f32)
        out_ref[j] = total.astype(bf16)


def fold_chunks(row, accum, parts, chunks, tokens):
    _, rows, width = parts.shape
    return pl.pallas_call(
        functools.partial(fold_chunks_kernel, tokens=float(tokens)),
        in_specs=[pl.BlockSpec(memory_space=pltpu.SMEM)] + [vmem_spec()] * 2,
        out_specs=vmem_spec(),
        out_shape=jax.ShapeDtypeStruct((chunks, rows, width // chunks), bf16),
        compiler_params=pltpu.CompilerParams(vmem_limit_bytes=VMEM_BYTES),
        name="fold_chunks",
    )(row, accum, parts)


def square_kernel(count_ref, sums_ref, square_ref, *, tokens):
    chunks, rows, width = sums_ref.shape
    square = jnp.zeros((rows, width), f32)
    for j in range(chunks):
        total = sums_ref[j].astype(f32) * (1.0 / tokens)
        square = square + total * total
    square_ref[...] = jnp.full(square_ref.shape, jnp.sum(square) * count_ref[0].astype(f32), f32)


def square_of(count, sums, tokens, peers):
    return pl.pallas_call(
        functools.partial(square_kernel, tokens=tokens),
        in_specs=[pl.BlockSpec(memory_space=pltpu.SMEM), vmem_spec()],
        out_specs=vmem_spec(),
        out_shape=jax.ShapeDtypeStruct((peers, 1, 128), f32),
        compiler_params=pltpu.CompilerParams(vmem_limit_bytes=VMEM_BYTES),
        name="square_of",
    )(count, sums)


def adam(total_grad, master, moment1, moment2, clip_factor):
    clipped = clip_factor * total_grad
    moment_one = beta_one * moment1 + (1.0 - beta_one) * clipped
    moment_two = beta_two * moment2 + (1.0 - beta_two) * clipped * clipped
    step = moment_one / bias_one / (jnp.sqrt(moment_two / bias_two) + epsilon) + decay_rate * master
    return step, master - learn_rate * step


def fresh_kernel(squares_ref, sums_ref, state_ref, out_ref, factor_ref, *, tokens):
    square_norm = jnp.sum(squares_ref[...], axis=0)
    clip_factor = jnp.minimum(1.0, clip_norm / jnp.sqrt(square_norm))
    factor_ref[...] = jnp.broadcast_to(clip_factor, factor_ref.shape)
    lanes = factor_ref.shape[1]
    width = sums_ref.shape[2]
    for j in range(out_ref.shape[2] // lanes):
        cols = slice(j * lanes, (j + 1) * lanes)
        within = slice(j * lanes % width, j * lanes % width + lanes)
        total = sums_ref[j * lanes // width, :, within].astype(f32) * (1.0 / tokens)
        fresh = adam(
            total, state_ref[0, :, cols], state_ref[1, :, cols], state_ref[2, :, cols], clip_factor
        )[1].astype(bf16)
        for copy in range(out_ref.shape[0]):
            out_ref[copy, :, cols] = fresh


def fresh_weights(squares, sums, state, tokens, copies):
    chunks, rows, width = sums.shape
    return pl.pallas_call(
        functools.partial(fresh_kernel, tokens=tokens),
        in_specs=[vmem_spec()] * 3,
        out_specs=[vmem_spec()] * 2,
        out_shape=[
            jax.ShapeDtypeStruct((copies, rows, chunks * width), bf16),
            jax.ShapeDtypeStruct((8, 128), f32),
        ],
        compiler_params=pltpu.CompilerParams(vmem_limit_bytes=VMEM_BYTES),
        name="fresh_weights",
    )(squares, sums, state)


def place_kernel(side_ref, order_ref, half_ref, *refs):
    out_ref = refs[-1]
    out_ref[...] = dot(order_ref[...], half_ref[...], ((1,), (0,))).astype(bf16)


def place(side, order, values, steps, into=None):
    slab, half = values.shape
    block = half // steps
    rest = [] if into is None else [into]
    return pl.pallas_call(
        place_kernel,
        grid_spec=pltpu.PrefetchScalarGridSpec(
            num_scalar_prefetch=1,
            grid=(steps,),
            in_specs=[
                pl.BlockSpec((slab, slab), lambda j, c: (0, 0)),
                pl.BlockSpec((slab, block), lambda j, c: (0, j)),
            ]
            + [pl.BlockSpec(memory_space=pl.ANY)] * len(rest),
            out_specs=pl.BlockSpec((slab, block), lambda j, c: (0, c[0] * steps + j)),
        ),
        out_shape=jax.ShapeDtypeStruct((slab, 2 * half), bf16),
        input_output_aliases={3: 0} if rest else {},
        cost_estimate=pl.CostEstimate(
            flops=2 * slab * slab * half, bytes_accessed=4 * slab * half, transcendentals=0
        ),
        compiler_params=pltpu.CompilerParams(vmem_limit_bytes=VMEM_BYTES),
        name="place",
    )(side, order, values, *rest)


def down(x, by):
    return lax.ppermute(x, "pipe", [(i, i - by) for i in range(by, 4)])


def swap(x, axis):
    return lax.ppermute(x, axis, [(0, 1), (1, 0)])


def local(top_grad, slab_inputs, weights, master, moment1, moment2, grad_accum, layer_counts):
    sizes = [lax.axis_size(axis) for axis in DP_AXES]
    n_y, n_z, n_x, n_core = sizes
    section = lax.axis_index("pipe").astype(jnp.int32)
    core = lax.axis_index("core").astype(jnp.int32)
    rows, width = top_grad.shape
    slab = slab_inputs.shape[2]
    span = 4 * slab
    half = width // 2
    tokens = rows * n_y * n_z * n_x * n_core
    slab_own, weight = slab_inputs[0], weights[0]
    shard = master.shape[1:]

    shares = [master[0], moment1[0], moment2[0], grad_accum[0]]
    known, one, two, three, sent, state = known_part(
        section[None], core[None], top_grad, weight, slab_own, shares, span, 4
    )
    state = lax.all_gather(state, "z", axis=0, tiled=False)
    known_all = [known, down(one, 1), down(two, 2), down(three, 3)]
    other = swap(sent, "core")
    w_head = lax.optimization_barrier((weight, known))[0][:, :span]

    here = jnp.arange(slab)
    source = here // (n_x * n_z) * (n_x * n_z) + here % n_z * n_x + here // n_z % n_x
    order = (here[None, :] == source[:, None]).astype(bf16)
    tail, slab_a, slab_b = tail_product(core[None], order, slab_own, top_grad, other, span)

    head, section_grad = relay(section[None], top_grad, known_all, w_head, slab, span)
    head_other = swap(head, "core")
    product = head_product(core[None], slab_a, slab_b, head, head_other, top_grad, other, tail)
    parts = lax.all_to_all(product, ("y", "x"), split_axis=0, concat_axis=0, tiled=True)
    row = lax.axis_index("z").astype(jnp.int32)
    parts = fold_chunks(
        row[None],
        grad_accum[0].reshape(1, half),
        parts.reshape(n_y * n_x, n_z, half),
        n_z,
        tokens,
    )
    parts = lax.all_to_all(parts, "z", split_axis=0, concat_axis=0, tiled=True)
    sums = lax.all_to_all(fold(parts), "z", split_axis=0, concat_axis=0, tiled=True)

    group = ("pipe", "y", "x", "core")
    count = lax.dynamic_slice(layer_counts, (section,), (1,))
    squares = square_of(count, sums, tokens, lax.axis_size(group))
    squares = lax.all_to_all(squares, group, split_axis=0, concat_axis=0, tiled=True)

    state = state.transpose(1, 0, 2, 3).reshape(8, n_z, half)
    fresh, factor = fresh_weights(squares, sums, state[:3], tokens, n_y * n_x)
    fresh = lax.all_to_all(fresh, ("y", "x"), split_axis=0, concat_axis=0, tiled=True)
    own = lax.dynamic_slice(sums, (0, row, 0), (n_z, 1, half // n_z)).astype(f32).reshape(shard) / tokens
    adam_step, new_master = adam(own, master[0], moment1[0], moment2[0], factor[0, 0])
    fresh, adam_step, new_master = lax.optimization_barrier((fresh, adam_step, new_master))
    fresh = fresh.reshape(slab, half)
    source = here // (n_x * n_z) * (n_x * n_z) + here % n_x * n_z + here // n_x % n_z
    order = (here[None, :] == source[:, None]).astype(bf16)
    fresh_other = swap(fresh, "core")
    new_weights = place(core[None], order, fresh, 2)
    new_weights = place(1 - core[None], order, fresh_other, 2, new_weights)

    return (new_weights[None], adam_step[None], new_master[None], section_grad[None])


def solution(mesh):
    devices = mesh.devices
    split = Mesh(devices.reshape((devices.shape[0],) + DP_SIZES), ("pipe",) + DP_AXES)
    return jax.shard_map(
        local,
        mesh=split,
        in_specs=(
            P(DP_AXES, None),
            P("pipe", DP_AXES, None),
            P("pipe", None, None),
            P("pipe", DP_AXES, None),
            P("pipe", DP_AXES, None),
            P("pipe", DP_AXES, None),
            P("pipe", DP_AXES, None),
            P(),
        ),
        out_specs=(
            P("pipe", None, None),
            P("pipe", DP_AXES, None),
            P("pipe", DP_AXES, None),
            P("pipe", DP_AXES, None),
        ),
        check_vma=False,
    )
```

```python
import functools
import jax
import jax.numpy as jnp
from jax import lax
from jax.experimental import pallas as pl
from jax.experimental.pallas import tpu as pltpu
from jax.sharding import Mesh, PartitionSpec as P

beta_one = 0.9
beta_two = 0.95
bias_one = 1.0 - 0.9**20
bias_two = 1.0 - 0.95**20
epsilon = 1e-08
decay_rate = 0.1
learn_rate = 0.0003
clip_norm = 1.0

bf16 = jnp.bfloat16
f32 = jnp.float32
VMEM_BYTES = 16 * 2**20
DP_AXES = ("y", "z", "x", "core")
DP_SIZES = (2, 16, 4, 2)


def dot(a, b, dims):
    return lax.dot_general(a, b, (dims, ((), ())), preferred_element_type=f32)


def vmem_spec():
    return pl.BlockSpec(memory_space=pltpu.VMEM)


def known_kernel(section_ref, core_ref, top_ref, weight_ref, slab_ref, share_a, share_b, share_c, share_d, out_ref, one_ref, two_ref, three_ref, sent_ref, state_ref, tops_ref, weights_ref, sems, *, slab, span, steps):
    rows, width = tops_ref.shape
    block, half = width // steps, width // 2
    section, core = section_ref[0], core_ref[0]

    def copies(step):
        cols = pl.ds(step * block, block)
        return (
            pltpu.make_async_copy(top_ref.at[:, cols], tops_ref.at[:, cols], sems.at[0, step]),
            pltpu.make_async_copy(weight_ref.at[:, cols], weights_ref.at[:, cols], sems.at[1, step]),
        )

    for step in range(steps):
        for copy in copies(step):
            copy.start()
    sent_ref[:, half:] = slab_ref[...]
    for i, share in enumerate((share_a, share_b, share_c, share_d) * 2):
        state_ref[i] = share[...]
    for step in range(steps):
        for copy in copies(step):
            copy.wait()
        start, end = step * block, (step + 1) * block
        if step == 0:
            column = lax.broadcasted_iota(jnp.int32, (rows, span), 1)
            later = column >= (section + 1) * slab
            known = jnp.where(later, 0.0, tops_ref[:, :span].astype(f32)).astype(bf16)
            total = dot(known, weights_ref[:, :span], ((1,), (1,)))
            one_ref[:, : 2 * slab] = weights_ref[:, 2 * slab : span]
            two_ref[:, :slab] = weights_ref[:, 3 * slab : span]
            start = span
        if start < end:
            total = total + dot(tops_ref[:, start:end], weights_ref[:, start:end], ((1,), (1,)))
    high = total.astype(bf16)
    low = (total - high.astype(f32)).astype(bf16)
    out_ref[...] = total
    for ref in (one_ref, two_ref, three_ref):
        end = ref.shape[1]
        ref[:, end - 2 * slab : end - slab] = high
        ref[:, end - slab :] = low

    @pl.when(core == 0)
    def _():
        sent_ref[:, :half] = tops_ref[:, half:]

    @pl.when(core != 0)
    def _():
        sent_ref[:, :half] = tops_ref[:, :half]


def known_part(section, core, top_grad, weight, slab_own, shares, span, steps):
    rows, width = top_grad.shape
    slab = slab_own.shape[1]
    widths = [slab, 4 * slab, 3 * slab, 2 * slab, width // 2 + slab]
    types = [f32, bf16, bf16, bf16, bf16]
    return pl.pallas_call(
        functools.partial(known_kernel, slab=slab, span=span, steps=steps),
        in_specs=[
            pl.BlockSpec(memory_space=pltpu.SMEM),
            pl.BlockSpec(memory_space=pltpu.SMEM),
            pl.BlockSpec(memory_space=pltpu.HBM),
            pl.BlockSpec(memory_space=pltpu.HBM),
        ]
        + [vmem_spec()] * 5,
        out_specs=[vmem_spec()] * 6,
        out_shape=[jax.ShapeDtypeStruct((rows, w), t) for w, t in zip(widths, types)]
        + [jax.ShapeDtypeStruct((8,) + shares[0].shape, f32)],
        scratch_shapes=[
            pltpu.VMEM((rows, width), bf16),
            pltpu.VMEM((slab, width), bf16),
            pltpu.SemaphoreType.DMA((2, steps)),
        ],
        compiler_params=pltpu.CompilerParams(vmem_limit_bytes=56 * 2**20),
        name="known_part",
    )(section, core, top_grad, weight, slab_own, *shares)


def relay_kernel(section_ref, top_ref, own_ref, one_ref, two_ref, three_ref, w_own_ref, head_ref, grad_ref, *, slab):
    section = section_ref[0]

    def pair(ref):
        end = ref.shape[1]
        return ref[:, end - 2 * slab : end - slab].astype(f32) + ref[:, end - slab :].astype(f32)

    for u in range(3, -1, -1):
        @pl.when(section <= u)
        def _(u=u):
            offset = u - section
            total = pair(three_ref)
            total = jnp.where(offset == 2, pair(two_ref), total)
            total = jnp.where(offset == 1, pair(one_ref), total)
            total = jnp.where(offset == 0, own_ref[...], total)
            for v in range(u + 1, 4):
                block = slice(v * slab, (v + 1) * slab)
                weight = w_own_ref[:, block].astype(f32)
                if v >= 2:
                    narrow = slice((v - 2) * slab, (v - 1) * slab)
                    weight = jnp.where(offset == 1, one_ref[:, narrow].astype(f32), weight)
                if v == 3:
                    weight = jnp.where(offset == 2, two_ref[:, :slab].astype(f32), weight)
                total = total + dot(head_ref[:, block], weight.astype(bf16), ((1,), (1,)))
            branch = total.astype(bf16)
            here = slice(u * slab, (u + 1) * slab)
            top = top_ref[:, here]
            placed = (top.astype(f32) + branch.astype(f32)).astype(bf16)
            head_ref[:, here] = jnp.where(offset == 0, top.astype(f32), placed.astype(f32)).astype(bf16)
            grad_ref[...] = branch

        @pl.when(section > u)
        def _(u=u):
            here = slice(u * slab, (u + 1) * slab)
            head_ref[:, here] = top_ref[:, here]


def relay(section, top_grad, known, weight, slab, span):
    rows = top_grad.shape[0]
    first = pl.BlockSpec((rows, span), lambda i: (0, 0))
    return pl.pallas_call(
        functools.partial(relay_kernel, slab=slab),
        grid=(1,),
        in_specs=[pl.BlockSpec(memory_space=pltpu.SMEM), first]
        + [pl.BlockSpec(k.shape, lambda i: (0, 0)) for k in known]
        + [pl.BlockSpec((slab, span), lambda i: (0, 0))],
        out_specs=[first, pl.BlockSpec((rows, slab), lambda i: (0, 0))],
        out_shape=[
            jax.ShapeDtypeStruct((rows, span), bf16),
            jax.ShapeDtypeStruct((rows, slab), bf16),
        ],
        compiler_params=pltpu.CompilerParams(vmem_limit_bytes=VMEM_BYTES),
        name="relay",
    )(section, top_grad, *known, weight)


def turn_kernel(order_ref, a_in_ref, b_in_ref, a_ref, b_ref):
    a_ref[...] = dot(order_ref[...], a_in_ref[...], ((1,), (1,))).astype(bf16)
    b_ref[...] = dot(order_ref[...], b_in_ref[...], ((1,), (1,))).astype(bf16)


def tail_kernel(core_ref, order_ref, slab_a_ref, slab_b_ref, top_ref, other_ref, out_ref, a_ref, b_ref):
    @pl.when(pl.program_id(0) == 0)
    def _():
        turn_kernel(order_ref, slab_a_ref, slab_b_ref, a_ref, b_ref)

    out_ref[...] = (
        dot(a_ref[...], top_ref[...], ((1,), (0,))) + dot(b_ref[...], other_ref[...], ((1,), (0,)))
    ).astype(bf16)


def tail_product(core, order, slab_a, top_grad, other, span):
    rows, width = top_grad.shape
    slab = slab_a.shape[1]
    half = width // 2
    blocks = half // span
    whole = pl.BlockSpec((rows, slab), lambda i, c: (0, 0))
    turned = pl.BlockSpec((slab, rows), lambda i, c: (0, 0))
    return pl.pallas_call(
        tail_kernel,
        grid_spec=pltpu.PrefetchScalarGridSpec(
            num_scalar_prefetch=1,
            grid=(blocks - 1,),
            in_specs=[
                turned,
                whole,
                pl.BlockSpec((rows, slab), lambda i, c: (0, half // slab)),
                pl.BlockSpec((rows, span), lambda i, c: (0, c[0] * blocks + i + 1)),
                pl.BlockSpec((rows, span), lambda i, c: (0, i + 1)),
            ],
            out_specs=[pl.BlockSpec((slab, span), lambda i, c: (0, i + 1)), turned, turned],
        ),
        out_shape=[
            jax.ShapeDtypeStruct((slab, half), bf16),
            jax.ShapeDtypeStruct((slab, rows), bf16),
            jax.ShapeDtypeStruct((slab, rows), bf16),
        ],
        compiler_params=pltpu.CompilerParams(vmem_limit_bytes=VMEM_BYTES),
        name="tail_product",
    )(core, order, slab_a, other, top_grad, other)


def head_kernel(core_ref, a_ref, b_ref, head_a_ref, head_b_ref, top_ref, other_ref, tail_ref, out_ref):
    @pl.when(core_ref[0] == 0)
    def _():
        out_ref[...] = (
            dot(a_ref[...], head_a_ref[...], ((1,), (0,))) + dot(b_ref[...], head_b_ref[...], ((1,), (0,)))
        ).astype(bf16)

    @pl.when(core_ref[0] != 0)
    def _():
        out_ref[...] = (
            dot(a_ref[...], top_ref[...], ((1,), (0,))) + dot(b_ref[...], other_ref[...], ((1,), (0,)))
        ).astype(bf16)


def head_product(core, a, b, head_a, head_b, top_grad, other, tail):
    rows, span = head_a.shape
    slab = a.shape[0]
    blocks = top_grad.shape[1] // 2 // span
    turned = pl.BlockSpec((slab, rows), lambda i, c: (0, 0))
    first = pl.BlockSpec((rows, span), lambda i, c: (0, 0))
    return pl.pallas_call(
        head_kernel,
        grid_spec=pltpu.PrefetchScalarGridSpec(
            num_scalar_prefetch=1,
            grid=(1,),
            in_specs=[turned, turned, first, first, pl.BlockSpec((rows, span), lambda i, c: (0, c[0] * blocks)), first]
            + [pl.BlockSpec(memory_space=pl.ANY)],
            out_specs=pl.BlockSpec((slab, span), lambda i, c: (0, 0)),
        ),
        out_shape=jax.ShapeDtypeStruct(tail.shape, bf16),
        input_output_aliases={7: 0},
        compiler_params=pltpu.CompilerParams(vmem_limit_bytes=VMEM_BYTES),
        name="head_product",
    )(core, a, b, head_a, head_b, top_grad, other, tail)


def fold_kernel(parts_ref, out_ref, *, count):
    total = parts_ref[0].astype(f32)
    for i in range(1, count):
        total = total + parts_ref[i].astype(f32)
    for i in range(count):
        out_ref[i] = total.astype(bf16)


def fold(parts):
    return pl.pallas_call(
        functools.partial(fold_kernel, count=parts.shape[0]),
        in_specs=[vmem_spec()],
        out_specs=vmem_spec(),
        out_shape=jax.ShapeDtypeStruct(parts.shape, bf16),
        compiler_params=pltpu.CompilerParams(vmem_limit_bytes=VMEM_BYTES),
        name="fold",
    )(parts)


def fold_chunks_kernel(row_ref, accum_ref, parts_ref, out_ref, *, tokens):
    count, rows, _ = parts_ref.shape
    chunks, _, width = out_ref.shape
    own = lax.broadcasted_iota(jnp.int32, (rows, width), 0) == row_ref[0]
    for j in range(chunks):
        cols = slice(j * width, (j + 1) * width)
        total = jnp.where(own, accum_ref[:, cols] * tokens, 0.0)
        for i in range(count):
            total = total + parts_ref[i, :, cols].astype(f32)
        out_ref[j] = total.astype(bf16)


def fold_chunks(row, accum, parts, chunks, tokens):
    _, rows, width = parts.shape
    return pl.pallas_call(
        functools.partial(fold_chunks_kernel, tokens=float(tokens)),
        in_specs=[pl.BlockSpec(memory_space=pltpu.SMEM)] + [vmem_spec()] * 2,
        out_specs=vmem_spec(),
        out_shape=jax.ShapeDtypeStruct((chunks, rows, width // chunks), bf16),
        compiler_params=pltpu.CompilerParams(vmem_limit_bytes=VMEM_BYTES),
        name="fold_chunks",
    )(row, accum, parts)


def square_kernel(count_ref, sums_ref, square_ref, *, tokens):
    chunks, rows, width = sums_ref.shape
    square = jnp.zeros((rows, width), f32)
    for j in range(chunks):
        total = sums_ref[j].astype(f32) * (1.0 / tokens)
        square = square + total * total
    square_ref[...] = jnp.full(square_ref.shape, jnp.sum(square) * count_ref[0].astype(f32), f32)


def square_of(count, sums, tokens, peers):
    return pl.pallas_call(
        functools.partial(square_kernel, tokens=tokens),
        in_specs=[pl.BlockSpec(memory_space=pltpu.SMEM), vmem_spec()],
        out_specs=vmem_spec(),
        out_shape=jax.ShapeDtypeStruct((peers, 1, 128), f32),
        compiler_params=pltpu.CompilerParams(vmem_limit_bytes=VMEM_BYTES),
        name="square_of",
    )(count, sums)


def adam(total_grad, master, moment1, moment2, clip_factor):
    clipped = clip_factor * total_grad
    moment_one = beta_one * moment1 + (1.0 - beta_one) * clipped
    moment_two = beta_two * moment2 + (1.0 - beta_two) * clipped * clipped
    step = moment_one / bias_one / (jnp.sqrt(moment_two / bias_two) + epsilon) + decay_rate * master
    return step, master - learn_rate * step


def fresh_kernel(squares_ref, sums_ref, state_ref, out_ref, factor_ref, *, tokens):
    square_norm = jnp.sum(squares_ref[...], axis=0)
    clip_factor = jnp.minimum(1.0, clip_norm / jnp.sqrt(square_norm))
    factor_ref[...] = jnp.broadcast_to(clip_factor, factor_ref.shape)
    lanes = factor_ref.shape[1]
    width = sums_ref.shape[2]
    for j in range(out_ref.shape[2] // lanes):
        cols = slice(j * lanes, (j + 1) * lanes)
        within = slice(j * lanes % width, j * lanes % width + lanes)
        total = sums_ref[j * lanes // width, :, within].astype(f32) * (1.0 / tokens)
        fresh = adam(
            total, state_ref[0, :, cols], state_ref[1, :, cols], state_ref[2, :, cols], clip_factor
        )[1].astype(bf16)
        for copy in range(out_ref.shape[0]):
            out_ref[copy, :, cols] = fresh


def fresh_weights(squares, sums, state, tokens, copies):
    chunks, rows, width = sums.shape
    return pl.pallas_call(
        functools.partial(fresh_kernel, tokens=tokens),
        in_specs=[vmem_spec()] * 3,
        out_specs=[vmem_spec()] * 2,
        out_shape=[
            jax.ShapeDtypeStruct((copies, rows, chunks * width), bf16),
            jax.ShapeDtypeStruct((8, 128), f32),
        ],
        compiler_params=pltpu.CompilerParams(vmem_limit_bytes=VMEM_BYTES),
        name="fresh_weights",
    )(squares, sums, state)


def place_kernel(side_ref, order_ref, half_ref, *refs):
    out_ref = refs[-1]
    out_ref[...] = dot(order_ref[...], half_ref[...], ((1,), (0,))).astype(bf16)


def place(side, order, values, steps, into=None):
    slab, half = values.shape
    block = half // steps
    rest = [] if into is None else [into]
    return pl.pallas_call(
        place_kernel,
        grid_spec=pltpu.PrefetchScalarGridSpec(
            num_scalar_prefetch=1,
            grid=(steps,),
            in_specs=[
                pl.BlockSpec((slab, slab), lambda j, c: (0, 0)),
                pl.BlockSpec((slab, block), lambda j, c: (0, j)),
            ]
            + [pl.BlockSpec(memory_space=pl.ANY)] * len(rest),
            out_specs=pl.BlockSpec((slab, block), lambda j, c: (0, c[0] * steps + j)),
        ),
        out_shape=jax.ShapeDtypeStruct((slab, 2 * half), bf16),
        input_output_aliases={3: 0} if rest else {},
        cost_estimate=pl.CostEstimate(
            flops=2 * slab * slab * half, bytes_accessed=4 * slab * half, transcendentals=0
        ),
        compiler_params=pltpu.CompilerParams(vmem_limit_bytes=VMEM_BYTES),
        name="place",
    )(side, order, values, *rest)


def down(x, by):
    return lax.ppermute(x, "pipe", [(i, i - by) for i in range(by, 4)])


def swap(x, axis):
    return lax.ppermute(x, axis, [(0, 1), (1, 0)])


def local(top_grad, slab_inputs, weights, master, moment1, moment2, grad_accum, layer_counts):
    sizes = [lax.axis_size(axis) for axis in DP_AXES]
    n_y, n_z, n_x, n_core = sizes
    section = lax.axis_index("pipe").astype(jnp.int32)
    core = lax.axis_index("core").astype(jnp.int32)
    rows, width = top_grad.shape
    slab = slab_inputs.shape[2]
    span = 4 * slab
    half = width // 2
    tokens = rows * n_y * n_z * n_x * n_core
    slab_own, weight = slab_inputs[0], weights[0]
    shard = master.shape[1:]

    shares = [master[0], moment1[0], moment2[0], grad_accum[0]]
    known, one, two, three, sent, state = known_part(
        section[None], core[None], top_grad, weight, slab_own, shares, span, 4
    )
    state = lax.all_gather(state, "z", axis=0, tiled=False)
    known_all = [known * (section >= 0).astype(f32), down(one, 1), down(two, 2), down(three, 3)]
    other = swap(sent, "core")
    w_head = lax.optimization_barrier((weight, known))[0][:, :span]

    here = jnp.arange(slab)
    source = here // (n_x * n_z) * (n_x * n_z) + here % n_z * n_x + here // n_z % n_x
    order = (here[None, :] == source[:, None]).astype(bf16)
    tail, slab_a, slab_b = tail_product(core[None], order, slab_own, top_grad, other, span)

    head, section_grad = relay(section[None], top_grad, known_all, w_head, slab, span)
    head_other = swap(head, "core")
    product = head_product(core[None], slab_a, slab_b, head, head_other, top_grad, other, tail)
    parts = lax.all_to_all(product, ("y", "x"), split_axis=0, concat_axis=0, tiled=True)
    row = lax.axis_index("z").astype(jnp.int32)
    parts = fold_chunks(
        row[None],
        grad_accum[0].reshape(1, half),
        parts.reshape(n_y * n_x, n_z, half),
        n_z,
        tokens,
    )
    parts = lax.all_to_all(parts, "z", split_axis=0, concat_axis=0, tiled=True)
    sums = lax.all_to_all(fold(parts), "z", split_axis=0, concat_axis=0, tiled=True)

    group = ("pipe", "y", "x", "core")
    count = lax.dynamic_slice(layer_counts, (section,), (1,))
    squares = square_of(count, sums, tokens, lax.axis_size(group))
    squares = lax.all_to_all(squares, group, split_axis=0, concat_axis=0, tiled=True)

    state = state.transpose(1, 0, 2, 3).reshape(8, n_z, half)
    fresh, factor = fresh_weights(squares, sums, state[:3], tokens, n_y * n_x)
    fresh = lax.all_to_all(fresh, ("y", "x"), split_axis=0, concat_axis=0, tiled=True)
    own = lax.dynamic_slice(sums, (0, row, 0), (n_z, 1, half // n_z)).astype(f32).reshape(shard) / tokens
    adam_step, new_master = adam(own, master[0], moment1[0], moment2[0], factor[0, 0])
    fresh, adam_step, new_master = lax.optimization_barrier((fresh, adam_step, new_master))
    fresh = fresh.reshape(slab, half)
    source = here // (n_x * n_z) * (n_x * n_z) + here % n_x * n_z + here // n_x % n_z
    order = (here[None, :] == source[:, None]).astype(bf16)
    fresh_other = swap(fresh, "core")
    new_weights = place(core[None], order, fresh, 2)
    new_weights = place(1 - core[None], order, fresh_other, 2, new_weights)

    return (new_weights[None], adam_step[None], new_master[None], section_grad[None])


def solution(mesh):
    devices = mesh.devices
    split = Mesh(devices.reshape((devices.shape[0],) + DP_SIZES), ("pipe",) + DP_AXES)
    return jax.shard_map(
        local,
        mesh=split,
        in_specs=(
            P(DP_AXES, None),
            P("pipe", DP_AXES, None),
            P("pipe", None, None),
            P("pipe", DP_AXES, None),
            P("pipe", DP_AXES, None),
            P("pipe", DP_AXES, None),
            P("pipe", DP_AXES, None),
            P(),
        ),
        out_specs=(
            P("pipe", None, None),
            P("pipe", DP_AXES, None),
            P("pipe", DP_AXES, None),
            P("pipe", DP_AXES, None),
        ),
        check_vma=False,
    )
```
